256 devices in a mesh: tm: 64 (over y_hi, z, x), col: 4 (over y_lo, core).
Axes of the slice: x: 4, y: 4 (y_hi: 2, y_lo: 2; y = y_hi * 2 + y_lo), z: 8, core: 2. Of those that a mesh axis runs over, the one named last changes fastest.
Arguments:
- near_prop: bfloat16 [128, 2, 512, 512], P('tm', None, None, 'col'), may hold values from -0.1875 to 0.1875
- far_prop: bfloat16 [128, 2, 512, 512], P('tm', None, None, 'col'), may hold values from -0.1875 to 0.1875
- meson: bfloat16 [128, 2, 512, 512], P('tm', None, None, 'col'), may hold values from -6 to 6
Outputs:
- blocks: float32 [128, 2, 512, 512], P('tm', None, None, 'col')
The draws below stay inside these ranges and needn't reach their ends.
All inputs are finite; a program needn't handle non-finite values.
Results may differ from the reference program's by a relative error of at most 0.0035.
Values may be sent and summed in bfloat16 or wider, within the bound.
No kernel may reach another device: no remote copies, remote signals or barrier semaphores. Data moves between devices by JAX's collectives and lax.ppermute only.
A program may use at most 64 MiB of HBM per device.

```python
import jax
import jax.numpy as jnp
from jax import lax

NO = 512
TIMES = 128
SEP_NEAR = 16
SEP_FAR = 48


def block_levels(stream_key, shape, shards, least, high):
    level = 1.0
    for dim, blocks in shards:
        heights = jax.random.uniform(jax.random.fold_in(jax.random.fold_in(stream_key, 6), dim), (blocks,), jnp.float32, least / len(shards), high / len(shards))
        level = level * jnp.repeat(jnp.exp(heights), shape[dim] // blocks).reshape((-1,) + (1,) * (len(shape) - 1 - dim))
    return level


def gaussian(key, shape, scale, bound, shards=(), dtype=jnp.bfloat16):
    values = jax.random.normal(key, shape, jnp.float32) * scale
    if len(shards) > 0:
        values = block_levels(key, shape, shards, -0.22, 0.18) * values
    return jnp.clip(values, min=-bound, max=bound).astype(dtype)


def setup_inputs(seed: int = 0) -> dict:
    streams_of = jax.random.split(jax.random.key(seed), 4)
    near_prop = gaussian(streams_of[0], (TIMES, 2, NO, NO), (2 * NO) ** -0.5, 0.1875, ((0, 64), (3, 4)))
    far_prop = gaussian(streams_of[1], (TIMES, 2, NO, NO), (2 * NO) ** -0.5, 0.1875, ((0, 64), (3, 4)))
    meson = gaussian(streams_of[2], (TIMES, 2, NO, NO), 1.0, 6.0, ((0, 64), (3, 4)))
    return dict(near_prop=near_prop, far_prop=far_prop, meson=meson)


def complex_product(left, right):
    real_part = jnp.einsum("tik,tkj->tij", left[:, 0], right[:, 0], precision=lax.Precision.HIGHEST) - jnp.einsum("tik,tkj->tij", left[:, 1], right[:, 1], precision=lax.Precision.HIGHEST)
    imag_part = jnp.einsum("tik,tkj->tij", left[:, 0], right[:, 1], precision=lax.Precision.HIGHEST) + jnp.einsum("tik,tkj->tij", left[:, 1], right[:, 0], precision=lax.Precision.HIGHEST)
    return jnp.stack([real_part, imag_part], axis=1)


def to_half(value):
    rounded = value.astype(jnp.bfloat16)
    rounded = lax.optimization_barrier(rounded)
    return rounded.astype(jnp.float32)


def gamma_adjoint(perambulator):
    order = perambulator.shape[2]
    signs = jnp.where(jnp.arange(order) < order // 2, 1.0, -1.0).astype(jnp.float32)
    both_signs = signs[:, None] * signs[None, :]
    conjugate = jnp.stack([perambulator[:, 0], -perambulator[:, 1]], axis=1)
    return jnp.swapaxes(conjugate, 2, 3) * both_signs


def reference(near_prop, far_prop, meson):
    meson_full = meson.astype(jnp.float32)
    total = jnp.zeros(meson.shape, jnp.float32)
    for separation, perambulator in ((SEP_NEAR, near_prop), (SEP_FAR, far_prop)):
        prop_full = perambulator.astype(jnp.float32)
        adjoint = gamma_adjoint(prop_full)
        shifted = jnp.roll(meson_full, -separation, axis=0)
        ahead = to_half(complex_product(shifted, prop_full))
        total = total + complex_product(adjoint, ahead)
        inner = to_half(complex_product(meson_full, adjoint))
        backward = to_half(complex_product(prop_full, inner))
        total = total + jnp.roll(backward, separation, axis=0)
    return total
```

```python
import jax
import jax.numpy as jnp
from jax import lax
from jax.experimental import pallas as pl
from jax.experimental.pallas import tpu as pltpu
from jax.sharding import PartitionSpec as P


BF16, F32 = jnp.bfloat16, jnp.float32
NT = (((1,), (1,)), ((), ()))
NN = (((1,), (0,)), ((), ()))
TN = (((0,), (0,)), ((), ()))


def dot(a, b, dims):
    return lax.dot_general(a, b, dims, preferred_element_type=F32)


def block(at, width):
    return pl.ds(pl.multiple_of(at * width, width), width)


def backward_kernel(where, p0, p1, p2, p3, m0, m1, m2, m3, xa, xb, ya, yb, prop, meson, inner, back):
    width = p0.shape[-1]
    half = prop.shape[-1] // 2
    for place, (p, m) in enumerate(((p0, m0), (p1, m1), (p2, m2), (p3, m3))):
        at = where[place]
        sign = jnp.where(at < 2, 1.0, -1.0).astype(F32)
        prop[:, :, block(at, width)] = p[...]
        meson[:, :, block(at, width)] = (m[...].astype(F32) * sign).astype(BF16)
    pr, pi, mr, mi = prop[0], prop[1], meson[0], meson[1]
    inner[0] = (dot(mr, pr, NT) + dot(mi, pi, NT)).astype(BF16)
    inner[1] = (dot(mi, pr, NT) - dot(mr, pi, NT)).astype(BF16)
    ir, ii = inner[0], inner[1]
    for part, total in ((0, dot(pr, ir, NN) - dot(pi, ii, NN)), (1, dot(pr, ii, NN) + dot(pi, ir, NN))):
        back[part, :, :half] = total[:, :half].astype(BF16)
        back[part, :, half:] = -total[:, half:].astype(BF16)
    for place, out in enumerate((xa, xb, ya, yb)):
        out[...] = back[:, :, block(where[4 + place], width)]


def forward_kernel(where, p0, p1, p2, p3, m0, m1, m2, m3, kept, given, prop, meson, ahead, total):
    width = p0.shape[-1]
    half = prop.shape[-1] // 2
    for place, (p, m) in enumerate(((p0, m0), (p1, m1), (p2, m2), (p3, m3))):
        prop[:, :, block(where[place], width)] = p[...]
        meson[:, :, block(where[4 + place], width)] = m[...]
    pr, pi, mr, mi = prop[0], prop[1], meson[0], meson[1]
    for part, value in ((0, dot(mr, pr, NN) - dot(mi, pi, NN)), (1, dot(mr, pi, NN) + dot(mi, pr, NN))):
        ahead[part, :half] = value[:half].astype(BF16)
        ahead[part, half:] = -value[half:].astype(BF16)
    ar, ai = ahead[0], ahead[1]
    for part, value in ((0, dot(pr, ar, TN) + dot(pi, ai, TN)), (1, dot(pr, ai, TN) - dot(pi, ar, TN))):
        total[part, :half] = value[:half]
        total[part, half:] = -value[half:]
    for n in range(2):
        kept[n] = total[:, :, block(where[8 + n], width)]
        given[n] = total[:, :, block(where[10 + n], width)].astype(BF16)


def shards(near_prop, far_prop, meson):
    _, parts, order, width = meson.shape
    peers = lax.axis_size("tm")
    cols = lax.axis_size("col")
    steps = (peers // 8, 3 * peers // 8)
    j, q = lax.axis_index("tm"), lax.axis_index("col")
    c, k = q // 2, q % 2

    def level(row):
        return row // (peers // 2)

    def to_rows(sign, crossed):
        pairs = []
        for row in range(peers):
            for chip in range(2):
                for core in range(2):
                    target = core ^ crossed if sign < 0 else core
                    there = (row + sign * steps[target]) % peers
                    chip_there = chip ^ level(row) ^ level(there)
                    pairs.append((row * cols + 2 * chip + core, there * cols + 2 * chip_there + (core ^ crossed)))
        return pairs

    def in_row(array, by):
        return lax.ppermute(array, "col", [(i, i ^ by) for i in range(cols)])

    def out_of_row(array, sign, crossed):
        return lax.ppermute(array, ("tm", "col"), to_rows(sign, crossed))

    ours = c ^ level(j)
    theirs = 1 - ours

    def pick(array, at):
        return lax.dynamic_index_in_dim(array, at, 0, keepdims=False)

    def prop_at(near_core, at):
        return jnp.where(k == near_core, pick(near_prop, at), pick(far_prop, at))

    m_ours, m_theirs = pick(meson, ours), pick(meson, theirs)
    p_ours, p_sib = prop_at(0, ours), prop_at(1, ours)

    m_cross = in_row(m_theirs, 2)
    next_a = out_of_row(m_ours, -1, 0)
    next_b = out_of_row(m_ours, -1, 1)
    p_cross = in_row(jnp.stack([prop_at(0, theirs), prop_at(1, theirs)]), 2)
    local = in_row(jnp.stack([p_sib, m_ours]), 1)
    next_c = out_of_row(m_cross, -1, 0)
    next_d = out_of_row(m_cross, -1, 1)
    local_cross = in_row(jnp.stack([p_cross[1], m_cross]), 1)

    props = (p_ours, local[0], p_cross[0], local_cross[0])
    mesons = (m_ours, local[1], m_cross, local_cross[1])
    step = jnp.where(k == 0, steps[0], steps[1])
    to_chip = ours ^ level((j + step) % peers)
    x, y = 2 * (1 - to_chip), 2 * to_chip
    where_back = jnp.stack([q, q ^ 1, q ^ 2, q ^ 3, x + k, x + 1 - k, y + k, y + 1 - k]).astype(jnp.int32)
    piece = jax.ShapeDtypeStruct((parts, order, width), BF16)
    whole = pltpu.VMEM((parts, order, order), BF16)
    vmem, smem = pl.BlockSpec(memory_space=pltpu.VMEM), pl.BlockSpec(memory_space=pltpu.SMEM)
    product = 8 * order**3
    xa, xb, ya, yb = pl.pallas_call(
        backward_kernel,
        out_shape=[piece] * 4,
        in_specs=[smem] + [vmem] * 8,
        out_specs=[vmem] * 4,
        scratch_shapes=[whole] * 4,
        compiler_params=pltpu.CompilerParams(vmem_limit_bytes=40 * 2**20),
        cost_estimate=pl.CostEstimate(flops=2 * product, bytes_accessed=12 * parts * order * width * 2, transcendentals=0),
        name="backward",
    )(where_back, *props, *mesons)
    back_xa, back_xb = out_of_row(xa, 1, 0), out_of_row(xb, 1, 1)
    back_ya, back_yb = out_of_row(ya, 1, 0), out_of_row(yb, 1, 1)

    u, v = 2 * to_chip, 2 * (1 - to_chip)
    z, w = 2 * (1 - c), 2 * c
    where_next = jnp.stack(
        [q, q ^ 1, q ^ 2, q ^ 3, u + k, u + 1 - k, v + k, v + 1 - k, z + k, w + k, z + 1 - k, w + 1 - k]
    ).astype(jnp.int32)
    kept, given = pl.pallas_call(
        forward_kernel,
        out_shape=[
            jax.ShapeDtypeStruct((2, parts, order, width), F32),
            jax.ShapeDtypeStruct((2, parts, order, width), BF16),
        ],
        in_specs=[smem] + [vmem] * 8,
        out_specs=[vmem] * 2,
        scratch_shapes=[whole] * 3 + [pltpu.VMEM((parts, order, order), F32)],
        compiler_params=pltpu.CompilerParams(vmem_limit_bytes=40 * 2**20),
        cost_estimate=pl.CostEstimate(flops=2 * product, bytes_accessed=14 * parts * order * width * 2, transcendentals=0),
        name="forward",
    )(where_next, *props, next_a, next_b, next_c, next_d)
    ahead = kept + in_row(given, 1).astype(F32)

    sent = ahead[0] + back_xa.astype(F32) + back_xb.astype(F32)
    from_partner = in_row(sent.astype(BF16), 2)
    stay = ahead[1] + back_ya.astype(F32) + back_yb.astype(F32)
    first = jnp.where(ours == 0, stay, from_partner.astype(F32))
    second = jnp.where(ours == 0, from_partner.astype(F32), stay)
    return jnp.stack([first, second])


def solution(mesh):
    placed = (P("tm", None, None, "col"), P("tm", None, None, "col"), P("tm", None, None, "col"))
    return jax.shard_map(
        shards, mesh=mesh, in_specs=placed, out_specs=P("tm", None, None, "col"), check_vma=False
    )
```

```python
import jax
import jax.numpy as jnp
from jax import lax
from jax.experimental import pallas as pl
from jax.experimental.pallas import tpu as pltpu
from jax.sharding import PartitionSpec as P


BF16, F32 = jnp.bfloat16, jnp.float32
NT = (((1,), (1,)), ((), ()))
NN = (((1,), (0,)), ((), ()))
TN = (((0,), (0,)), ((), ()))


def dot(a, b, dims):
    return lax.dot_general(a, b, dims, preferred_element_type=F32)


def block(at, width):
    return pl.ds(pl.multiple_of(at * width, width), width)


def backward_kernel(where, p0, p1, p2, p3, m0, m1, m2, m3, x, y, prop, meson, inner, back):
    width = p0.shape[-1]
    half = prop.shape[-1] // 2
    for place, (p, m) in enumerate(((p0, m0), (p1, m1), (p2, m2), (p3, m3))):
        at = where[place]
        sign = jnp.where(at < 2, 1.0, -1.0).astype(F32)
        prop[:, :, block(at, width)] = p[...]
        meson[:, :, block(at, width)] = (m[...].astype(F32) * sign).astype(BF16)
    pr, pi, mr, mi = prop[0], prop[1], meson[0], meson[1]
    inner[0] = (dot(mr, pr, NT) + dot(mi, pi, NT)).astype(BF16)
    inner[1] = (dot(mi, pr, NT) - dot(mr, pi, NT)).astype(BF16)
    ir, ii = inner[0], inner[1]
    for part, total in ((0, dot(pr, ir, NN) - dot(pi, ii, NN)), (1, dot(pr, ii, NN) + dot(pi, ir, NN))):
        back[part, :, :half] = total[:, :half].astype(BF16)
        back[part, :, half:] = -total[:, half:].astype(BF16)
    for n in range(2):
        x[n] = back[:, :, block(where[4 + n], width)]
        y[n] = back[:, :, block(where[6 + n], width)]


def forward_kernel(where, p0, p1, p2, p3, m01, m23, kept_x, kept_y, given_x, given_y, prop, meson, ahead, total):
    width = p0.shape[-1]
    half = prop.shape[-1] // 2
    for place, p in enumerate((p0, p1, p2, p3)):
        prop[:, :, block(where[place], width)] = p[...]
    for n in range(2):
        meson[:, :, block(where[4 + n], width)] = m01[n]
        meson[:, :, block(where[6 + n], width)] = m23[n]
    pr, pi, mr, mi = prop[0], prop[1], meson[0], meson[1]
    for part, value in ((0, dot(mr, pr, NN) - dot(mi, pi, NN)), (1, dot(mr, pi, NN) + dot(mi, pr, NN))):
        ahead[part, :half] = value[:half].astype(BF16)
        ahead[part, half:] = -value[half:].astype(BF16)
    ar, ai = ahead[0], ahead[1]
    for part, value in ((0, dot(pr, ar, TN) + dot(pi, ai, TN)), (1, dot(pr, ai, TN) - dot(pi, ar, TN))):
        total[part, :half] = value[:half]
        total[part, half:] = -value[half:]
    for n, out in enumerate((kept_x, kept_y, given_x, given_y)):
        out[...] = total[:, :, block(where[8 + n], width)]


def shards(near_prop, far_prop, meson):
    _, parts, order, width = meson.shape
    peers = lax.axis_size("tm")
    cols = lax.axis_size("col")
    steps = (peers // 8, 3 * peers // 8)
    j, q = lax.axis_index("tm"), lax.axis_index("col")
    c, k = q >> 1, q & 1

    def level(row):
        return (row >= peers // 2) * 1

    def to_rows(sign, crossed):
        pairs = []
        for row in range(peers):
            for chip in range(2):
                for core in range(2):
                    target = core ^ crossed if sign < 0 else core
                    there = (row + sign * steps[target]) % peers
                    chip_there = chip ^ level(row) ^ level(there)
                    pairs.append((row * cols + 2 * chip + core, there * cols + 2 * chip_there + (core ^ crossed)))
        return pairs

    def in_row(array, by):
        return lax.ppermute(array, "col", [(i, i ^ by) for i in range(cols)])

    def out_of_row(array, sign, crossed):
        return lax.ppermute(array, ("tm", "col"), to_rows(sign, crossed))

    ours = c ^ level(j)
    theirs = 1 - ours

    def pick(array, at):
        return lax.dynamic_index_in_dim(array, at, 0, keepdims=False)

    def prop_at(near_core, at):
        return jnp.where(k == near_core, pick(near_prop, at), pick(far_prop, at))

    m_ours, m_theirs = pick(meson, ours), pick(meson, theirs)
    p_ours, p_sib = prop_at(0, ours), prop_at(1, ours)

    m_sib = in_row(m_ours, 1)
    next_1 = out_of_row(jnp.stack([m_ours, m_sib]), -1, 0)
    m_cross = in_row(m_theirs, 2)
    local = in_row(jnp.stack([p_sib, m_cross]), 1)
    next_2 = out_of_row(jnp.stack([m_cross, local[1]]), -1, 0)
    p_cross = in_row(jnp.stack([prop_at(0, theirs), prop_at(1, theirs)]), 2)
    p_cross, next_1 = lax.optimization_barrier((p_cross, next_1))
    p_last = in_row(p_cross[1], 1)

    props = (p_ours, local[0], p_cross[0], p_last)
    mesons = (m_ours, m_sib, m_cross, local[1])
    step = jnp.where(k == 0, steps[0], steps[1])
    to_chip = ours ^ level((j + step) & (peers - 1))
    x, y = 2 * (1 - to_chip), 2 * to_chip
    where_back = jnp.stack([q, q ^ 1, q ^ 2, q ^ 3, x + k, x + 1 - k, y + k, y + 1 - k]).astype(jnp.int32)
    piece = jax.ShapeDtypeStruct((2, parts, order, width), BF16)
    whole = pltpu.VMEM((parts, order, order), BF16)
    vmem, smem = pl.BlockSpec(memory_space=pltpu.VMEM), pl.BlockSpec(memory_space=pltpu.SMEM)
    product = 8 * order**3
    x_out, y_out = pl.pallas_call(
        backward_kernel,
        out_shape=[piece] * 2,
        in_specs=[smem] + [vmem] * 8,
        out_specs=[vmem] * 2,
        scratch_shapes=[whole] * 4,
        compiler_params=pltpu.CompilerParams(vmem_limit_bytes=40 * 2**20),
        cost_estimate=pl.CostEstimate(flops=1, bytes_accessed=1, transcendentals=0),
        name="backward",
    )(where_back, *props, *mesons)
    x_in, y_in = out_of_row(x_out, 1, 0), out_of_row(y_out, 1, 0)
    *late, x_out, y_out = lax.optimization_barrier((*props, x_out, y_out))

    u, v = 2 * to_chip, 2 * (1 - to_chip)
    z, w = 2 * (1 - c), 2 * c
    where_next = jnp.stack(
        [q, q ^ 1, q ^ 2, q ^ 3, u + k, u + 1 - k, v + k, v + 1 - k, z + k, w + k, z + 1 - k, w + 1 - k]
    ).astype(jnp.int32)
    kept_x, kept_y, given_x, given_y = pl.pallas_call(
        forward_kernel,
        out_shape=[jax.ShapeDtypeStruct((parts, order, width), F32)] * 4,
        in_specs=[smem] + [vmem] * 6,
        out_specs=[vmem] * 4,
        scratch_shapes=[whole] * 3 + [pltpu.VMEM((parts, order, order), F32)],
        compiler_params=pltpu.CompilerParams(vmem_limit_bytes=40 * 2**20),
        cost_estimate=pl.CostEstimate(flops=int(5 * product), bytes_accessed=14 * parts * order * width * 2, transcendentals=0),
        name="forward",
    )(where_next, *late, next_1, next_2)

    from_same = in_row((kept_x + x_in[0].astype(F32)).astype(BF16), 2)
    from_other = in_row((given_x + x_in[1].astype(F32)).astype(BF16), 3)
    y_in, from_same, from_other = lax.optimization_barrier((y_in, from_same, from_other))
    from_sib = in_row((given_y + y_in[1].astype(F32)).astype(BF16), 1)
    stay = kept_y + y_in[0].astype(F32) + from_sib.astype(F32)
    arrived = from_same.astype(F32) + from_other.astype(F32)
    first = jnp.where(ours == 0, stay, arrived)
    second = jnp.where(ours == 0, arrived, stay)
    return jnp.stack([first, second])


def solution(mesh):
    placed = (P("tm", None, None, "col"), P("tm", None, None, "col"), P("tm", None, None, "col"))
    return jax.shard_map(
        shards, mesh=mesh, in_specs=placed, out_specs=P("tm", None, None, "col"), check_vma=False
    )
```

```python
import jax
import jax.numpy as jnp
from jax import lax
from jax.experimental import pallas as pl
from jax.experimental.pallas import tpu as pltpu
from jax.sharding import PartitionSpec as P


BF16, F32 = jnp.bfloat16, jnp.float32
NT = (((1,), (1,)), ((), ()))
NN = (((1,), (0,)), ((), ()))
TN = (((0,), (0,)), ((), ()))


def dot(a, b, dims):
    return lax.dot_general(a, b, dims, preferred_element_type=F32)


def block(at, width):
    return pl.ds(pl.multiple_of(at * width, width), width)


def backward_kernel(where, p0, p1, p2, p3, m0, m1, m2, m3, x, y, prop, meson, inner, back):
    width = p0.shape[-1]
    half = prop.shape[-1] // 2
    for place, (p, m) in enumerate(((p0, m0), (p1, m1), (p2, m2), (p3, m3))):
        at = where[place]
        sign = jnp.where(at < 2, 1.0, -1.0).astype(F32)
        prop[:, :, block(at, width)] = p[...]
        meson[:, :, block(at, width)] = (m[...].astype(F32) * sign).astype(BF16)
    pr, pi, mr, mi = prop[0], prop[1], meson[0], meson[1]
    inner[0] = (dot(mr, pr, NT) + dot(mi, pi, NT)).astype(BF16)
    inner[1] = (dot(mi, pr, NT) - dot(mr, pi, NT)).astype(BF16)
    ir, ii = inner[0], inner[1]
    for part, total in ((0, dot(pr, ir, NN) - dot(pi, ii, NN)), (1, dot(pr, ii, NN) + dot(pi, ir, NN))):
        back[part, :, :half] = total[:, :half].astype(BF16)
        back[part, :, half:] = -total[:, half:].astype(BF16)
    for n in range(2):
        x[n] = back[:, :, block(where[4 + n], width)]
        y[n] = back[:, :, block(where[6 + n], width)]


def forward_kernel(where, p0, p1, p2, p3, m01, m23, kept_x, kept_y, given_x, given_y, prop, meson, ahead, total):
    width = p0.shape[-1]
    half = prop.shape[-1] // 2
    for place, p in enumerate((p0, p1, p2, p3)):
        prop[:, :, block(where[place], width)] = p[...]
    for n in range(2):
        meson[:, :, block(where[4 + n], width)] = m01[n]
        meson[:, :, block(where[6 + n], width)] = m23[n]
    pr, pi, mr, mi = prop[0], prop[1], meson[0], meson[1]
    for part, value in ((0, dot(mr, pr, NN) - dot(mi, pi, NN)), (1, dot(mr, pi, NN) + dot(mi, pr, NN))):
        ahead[part, :half] = value[:half].astype(BF16)
        ahead[part, half:] = -value[half:].astype(BF16)
    ar, ai = ahead[0], ahead[1]
    for part, value in ((0, dot(pr, ar, TN) + dot(pi, ai, TN)), (1, dot(pr, ai, TN) - dot(pi, ar, TN))):
        total[part, :half] = value[:half]
        total[part, half:] = -value[half:]
    for n, out in enumerate((kept_x, kept_y, given_x, given_y)):
        out[...] = total[:, :, block(where[8 + n], width)]


def shards(near_prop, far_prop, meson):
    _, parts, order, width = meson.shape
    peers = lax.axis_size("tm")
    cols = lax.axis_size("col")
    steps = (peers // 8, 3 * peers // 8)
    j, q = lax.axis_index("tm"), lax.axis_index("col")
    c, k = q >> 1, q & 1

    def level(row):
        return (row >= peers // 2) * 1

    def to_rows(sign, crossed):
        pairs = []
        for row in range(peers):
            for chip in range(2):
                for core in range(2):
                    target = core ^ crossed if sign < 0 else core
                    there = (row + sign * steps[target]) % peers
                    chip_there = chip ^ level(row) ^ level(there)
                    pairs.append((row * cols + 2 * chip + core, there * cols + 2 * chip_there + (core ^ crossed)))
        return pairs

    def in_row(array, by):
        return lax.ppermute(array, "col", [(i, i ^ by) for i in range(cols)])

    def out_of_row(array, sign, crossed):
        return lax.ppermute(array, ("tm", "col"), to_rows(sign, crossed))

    ours = c ^ level(j)
    theirs = 1 - ours

    def pick(array, at):
        return lax.dynamic_index_in_dim(array, at, 0, keepdims=False)

    def prop_at(near_core, at):
        return jnp.where(k == near_core, pick(near_prop, at), pick(far_prop, at))

    m_ours, m_theirs = pick(meson, ours), pick(meson, theirs)
    p_ours, p_sib = prop_at(0, ours), prop_at(1, ours)

    m_sib = in_row(m_ours, 1)
    next_1 = out_of_row(jnp.stack([m_ours, m_sib]), -1, 0)
    m_cross = in_row(m_theirs, 2)
    local = in_row(jnp.stack([p_sib, m_cross]), 1)
    next_1, local = lax.optimization_barrier((next_1, local))
    next_2 = out_of_row(jnp.stack([m_cross, local[1]]), -1, 0)
    p_cross = in_row(jnp.stack([prop_at(0, theirs), prop_at(1, theirs)]), 2)
    p_last = in_row(p_cross[1], 1)

    props = (p_ours, local[0], p_cross[0], p_last)
    mesons = (m_ours, m_sib, m_cross, local[1])
    step = jnp.where(k == 0, steps[0], steps[1])
    to_chip = ours ^ level((j + step) & (peers - 1))
    x, y = 2 * (1 - to_chip), 2 * to_chip
    where_back = jnp.stack([q, q ^ 1, q ^ 2, q ^ 3, x + k, x + 1 - k, y + k, y + 1 - k]).astype(jnp.int32)
    piece = jax.ShapeDtypeStruct((2, parts, order, width), BF16)
    whole = pltpu.VMEM((parts, order, order), BF16)
    vmem, smem = pl.BlockSpec(memory_space=pltpu.VMEM), pl.BlockSpec(memory_space=pltpu.SMEM)
    product = 8 * order**3
    x_out, y_out = pl.pallas_call(
        backward_kernel,
        out_shape=[piece] * 2,
        in_specs=[smem] + [vmem] * 8,
        out_specs=[vmem] * 2,
        scratch_shapes=[whole] * 4,
        compiler_params=pltpu.CompilerParams(vmem_limit_bytes=40 * 2**20),
        cost_estimate=pl.CostEstimate(flops=1, bytes_accessed=1, transcendentals=0),
        name="backward",
    )(where_back, *props, *mesons)
    x_in, y_in = out_of_row(x_out, 1, 0), out_of_row(y_out, 1, 0)
    *late, x_out, y_out = lax.optimization_barrier((*props, x_out, y_out))

    u, v = 2 * to_chip, 2 * (1 - to_chip)
    z, w = 2 * (1 - c), 2 * c
    where_next = jnp.stack(
        [q, q ^ 1, q ^ 2, q ^ 3, u + k, u + 1 - k, v + k, v + 1 - k, z + k, w + k, z + 1 - k, w + 1 - k]
    ).astype(jnp.int32)
    kept_x, kept_y, given_x, given_y = pl.pallas_call(
        forward_kernel,
        out_shape=[jax.ShapeDtypeStruct((parts, order, width), F32)] * 4,
        in_specs=[smem] + [vmem] * 6,
        out_specs=[vmem] * 4,
        scratch_shapes=[whole] * 3 + [pltpu.VMEM((parts, order, order), F32)],
        compiler_params=pltpu.CompilerParams(vmem_limit_bytes=40 * 2**20),
        cost_estimate=pl.CostEstimate(flops=5 * product, bytes_accessed=14 * parts * order * width * 2, transcendentals=0),
        name="forward",
    )(where_next, *late, next_1, next_2)

    from_sib = in_row((given_x + x_in[1].astype(F32)).astype(BF16), 1)
    sent = kept_x + x_in[0].astype(F32) + from_sib.astype(F32)
    from_partner = in_row(sent.astype(BF16), 2)
    y_in, from_partner = lax.optimization_barrier((y_in, from_partner))
    from_sib_y = in_row((given_y + y_in[1].astype(F32)).astype(BF16), 1)
    stay = kept_y + y_in[0].astype(F32) + from_sib_y.astype(F32)
    slot = lax.broadcasted_iota(jnp.int32, (2, parts, order, width), 0)
    return jnp.where(slot == ours, stay[None], from_partner.astype(F32)[None])


def solution(mesh):
    placed = (P("tm", None, None, "col"), P("tm", None, None, "col"), P("tm", None, None, "col"))
    return jax.shard_map(
        shards, mesh=mesh, in_specs=placed, out_specs=P("tm", None, None, "col"), check_vma=False
    )
```

```python
import jax
import jax.numpy as jnp
from jax import lax
from jax.experimental import pallas as pl
from jax.experimental.pallas import tpu as pltpu
from jax.sharding import PartitionSpec as P


BF16, F32 = jnp.bfloat16, jnp.float32
NT = (((1,), (1,)), ((), ()))
NN = (((1,), (0,)), ((), ()))
TN = (((0,), (0,)), ((), ()))


def dot(a, b, dims):
    return lax.dot_general(a, b, dims, preferred_element_type=F32)


def block(at, width):
    return pl.ds(pl.multiple_of(at * width, width), width)


def backward_kernel(where, p0, p1, p2, p3, m0, m1, m2, m3, x, y, prop, meson, inner, back):
    width = p0.shape[-1]
    half = prop.shape[-1] // 2
    for place, (p, m) in enumerate(((p0, m0), (p1, m1), (p2, m2), (p3, m3))):
        at = where[place]
        sign = jnp.where(at < 2, 1.0, -1.0).astype(F32)
        prop[:, :, block(at, width)] = p[...]
        meson[:, :, block(at, width)] = (m[...].astype(F32) * sign).astype(BF16)
    pr, pi, mr, mi = prop[0], prop[1], meson[0], meson[1]
    inner[0] = (dot(mr, pr, NT) + dot(mi, pi, NT)).astype(BF16)
    inner[1] = (dot(mi, pr, NT) - dot(mr, pi, NT)).astype(BF16)
    ir, ii = inner[0], inner[1]
    for part, total in ((0, dot(pr, ir, NN) - dot(pi, ii, NN)), (1, dot(pr, ii, NN) + dot(pi, ir, NN))):
        back[part, :, :half] = total[:, :half].astype(BF16)
        back[part, :, half:] = -total[:, half:].astype(BF16)
    for n in range(2):
        x[n] = back[:, :, block(where[4 + n], width)]
        y[n] = back[:, :, block(where[6 + n], width)]


def forward_kernel(where, p0, p1, p2, p3, m01, m23, kept_x, kept_y, given_x, given_y, prop, meson, ahead, total):
    width = p0.shape[-1]
    half = prop.shape[-1] // 2
    for place, p in enumerate((p0, p1, p2, p3)):
        prop[:, :, block(where[place], width)] = p[...]
    for n in range(2):
        meson[:, :, block(where[4 + n], width)] = m01[n]
        meson[:, :, block(where[6 + n], width)] = m23[n]
    pr, pi, mr, mi = prop[0], prop[1], meson[0], meson[1]
    for part, value in ((0, dot(mr, pr, NN) - dot(mi, pi, NN)), (1, dot(mr, pi, NN) + dot(mi, pr, NN))):
        ahead[part, :half] = value[:half].astype(BF16)
        ahead[part, half:] = -value[half:].astype(BF16)
    ar, ai = ahead[0], ahead[1]
    for part, value in ((0, dot(pr, ar, TN) + dot(pi, ai, TN)), (1, dot(pr, ai, TN) - dot(pi, ar, TN))):
        total[part, :half] = value[:half]
        total[part, half:] = -value[half:]
    for n, out in enumerate((kept_x, kept_y, given_x, given_y)):
        out[...] = total[:, :, block(where[8 + n], width)]


def second_kernel(pair, out):
    out[...] = pair[0]


def join_kernel(a, pair, out):
    out[...] = (a[...] + pair[0].astype(F32)).astype(BF16)


def in_rows(kernel, cost, *arrays):
    _, parts, order, width = arrays[-1].shape
    rows = order // 4
    flat = pl.BlockSpec((parts, rows, width), lambda i: (0, i, 0))
    pair = pl.BlockSpec((1, parts, rows, width), lambda i: (1, 0, i, 0))
    return pl.pallas_call(
        kernel,
        grid=(4,),
        out_shape=jax.ShapeDtypeStruct((parts, order, width), BF16),
        in_specs=[flat] * (len(arrays) - 1) + [pair],
        out_specs=flat,
        cost_estimate=pl.CostEstimate(flops=cost, bytes_accessed=1, transcendentals=0),
        name=kernel.__name__,
    )(*arrays)


def shards(near_prop, far_prop, meson):
    _, parts, order, width = meson.shape
    peers = lax.axis_size("tm")
    cols = lax.axis_size("col")
    steps = (peers // 8, 3 * peers // 8)
    j, q = lax.axis_index("tm"), lax.axis_index("col")
    c, k = q >> 1, q & 1

    def level(row):
        return (row >= peers // 2) * 1

    def to_rows(sign, crossed):
        pairs = []
        for row in range(peers):
            for chip in range(2):
                for core in range(2):
                    target = core ^ crossed if sign < 0 else core
                    there = (row + sign * steps[target]) % peers
                    chip_there = chip ^ level(row) ^ level(there)
                    pairs.append((row * cols + 2 * chip + core, there * cols + 2 * chip_there + (core ^ crossed)))
        return pairs

    def in_row(array, by):
        return lax.ppermute(array, "col", [(i, i ^ by) for i in range(cols)])

    def out_of_row(array, sign, crossed):
        return lax.ppermute(array, ("tm", "col"), to_rows(sign, crossed))

    ours = c ^ level(j)
    theirs = 1 - ours

    def pick(array, at):
        return lax.dynamic_index_in_dim(array, at, 0, keepdims=False)

    def prop_at(near_core, at):
        return jnp.where(k == near_core, pick(near_prop, at), pick(far_prop, at))

    m_ours, m_theirs = pick(meson, ours), pick(meson, theirs)
    p_ours, p_sib = prop_at(0, ours), prop_at(1, ours)

    p_from_sib, m_sib = in_row(jnp.stack([p_sib, m_ours]), 1)
    next_1 = out_of_row(jnp.stack([m_ours, m_sib]), -1, 0)
    m_cross = in_row(m_theirs, 2)
    m_last = in_row(m_cross, 1)
    next_2 = out_of_row(jnp.stack([m_cross, m_last]), -1, 0)
    p_cross = in_row(jnp.stack([prop_at(0, theirs), prop_at(1, theirs)]), 2)
    p_cross, next_1 = lax.optimization_barrier((p_cross, next_1))
    p_last = in_row(p_cross[1], 1)

    props = (p_ours, p_from_sib, p_cross[0], p_last)
    mesons = (m_ours, m_sib, m_cross, m_last)
    step = jnp.where(k == 0, steps[0], steps[1])
    to_chip = ours ^ level((j + step) & (peers - 1))
    x, y = 2 * (1 - to_chip), 2 * to_chip
    where_back = jnp.stack([q, q ^ 1, q ^ 2, q ^ 3, x + k, x + 1 - k, y + k, y + 1 - k]).astype(jnp.int32)
    piece = jax.ShapeDtypeStruct((2, parts, order, width), BF16)
    whole = pltpu.VMEM((parts, order, order), BF16)
    vmem, smem = pl.BlockSpec(memory_space=pltpu.VMEM), pl.BlockSpec(memory_space=pltpu.SMEM)
    product = 8 * order**3
    x_out, y_out = pl.pallas_call(
        backward_kernel,
        out_shape=[piece] * 2,
        in_specs=[smem] + [vmem] * 8,
        out_specs=[vmem] * 2,
        scratch_shapes=[whole] * 4,
        compiler_params=pltpu.CompilerParams(vmem_limit_bytes=40 * 2**20),
        cost_estimate=pl.CostEstimate(flops=1, bytes_accessed=1, transcendentals=0),
        name="backward",
    )(where_back, *props, *mesons)
    x_in, y_in = out_of_row(x_out, 1, 0), out_of_row(y_out, 1, 0)
    *late, x_out, y_out = lax.optimization_barrier((*props, x_out, y_out))

    u, v = 2 * to_chip, 2 * (1 - to_chip)
    z, w = 2 * (1 - c), 2 * c
    where_next = jnp.stack(
        [q, q ^ 1, q ^ 2, q ^ 3, u + k, u + 1 - k, v + k, v + 1 - k, z + k, w + k, z + 1 - k, w + 1 - k]
    ).astype(jnp.int32)
    kept_x, kept_y, given_x, given_y = pl.pallas_call(
        forward_kernel,
        out_shape=[jax.ShapeDtypeStruct((parts, order, width), F32)] * 4,
        in_specs=[smem] + [vmem] * 6,
        out_specs=[vmem] * 4,
        scratch_shapes=[whole] * 3 + [pltpu.VMEM((parts, order, order), F32)],
        compiler_params=pltpu.CompilerParams(vmem_limit_bytes=40 * 2**20),
        cost_estimate=pl.CostEstimate(flops=5 * product, bytes_accessed=14 * parts * order * width * 2, transcendentals=0),
        name="forward",
    )(where_next, *late, next_1, next_2)

    from_sib = in_row((given_x + x_in[1].astype(F32)).astype(BF16), 1)
    sent = kept_x + x_in[0].astype(F32) + from_sib.astype(F32)
    sent = sent.astype(BF16)
    y_in, held = lax.optimization_barrier((y_in, sent))
    from_partner = in_row(sent, 2)
    from_sib_y = in_row(in_rows(join_kernel, 1, given_y, y_in), 1)
    stay = kept_y + y_in[0].astype(F32)
    base = jnp.broadcast_to(from_partner.astype(F32)[None], (2, parts, order, width))
    base, stay, from_sib_y = lax.optimization_barrier((base, stay, from_sib_y))
    return lax.dynamic_update_index_in_dim(base, stay + from_sib_y.astype(F32), ours, 0)


def solution(mesh):
    placed = (P("tm", None, None, "col"), P("tm", None, None, "col"), P("tm", None, None, "col"))
    return jax.shard_map(
        shards, mesh=mesh, in_specs=placed, out_specs=P("tm", None, None, "col"), check_vma=False
    )
```

```python
import jax
import jax.numpy as jnp
from jax import lax
from jax.experimental import pallas as pl
from jax.experimental.pallas import tpu as pltpu
from jax.sharding import PartitionSpec as P


BF16, F32 = jnp.bfloat16, jnp.float32
NT = (((1,), (1,)), ((), ()))
NN = (((1,), (0,)), ((), ()))
TN = (((0,), (0,)), ((), ()))


def dot(a, b, dims):
    return lax.dot_general(a, b, dims, preferred_element_type=F32)


def block(at, width):
    return pl.ds(pl.multiple_of(at * width, width), width)


def backward_kernel(where, p0, p1, p2, p3, m0, m1, m2, m3, x, y, prop, meson, turned, inner, back, sems):
    order, width = prop.shape[0], p0.shape[-1]
    half = order // 2
    for place, (p, m) in enumerate(((p0, m0), (p1, m1), (p2, m2), (p3, m3))):
        at = where[place]
        sign = jnp.where(at < 2, 1.0, -1.0).astype(F32)
        real, imag = block(at, width), block(at + 4, width)
        mr, mi = m[0].astype(F32) * sign, m[1].astype(F32) * sign
        prop[:, real], prop[:, imag] = p[0], p[1]
        meson[:, real], meson[:, imag] = mr.astype(BF16), mi.astype(BF16)
        turned[:, real], turned[:, imag] = mi.astype(BF16), (-mr).astype(BF16)
    real, imag = dot(meson[...], prop[...], NT), dot(turned[...], prop[...], NT)
    inner[0, :order], inner[0, order:] = real.astype(BF16), (-imag).astype(BF16)
    inner[1, :order], inner[1, order:] = imag.astype(BF16), real.astype(BF16)
    copies = []
    for part in range(2):
        total = dot(prop[...], inner[part], NN)
        back[part, :, :half] = total[:, :half].astype(BF16)
        back[part, :, half:] = (-total[:, half:]).astype(BF16)
        for place, out in enumerate((x.at[0], x.at[1], y.at[0], y.at[1])):
            columns = block(where[4 + place], width)
            copies.append(pltpu.make_async_copy(back.at[part, :, columns], out.at[part], sems.at[part, place]))
            copies[-1].start()
    for copy in copies:
        copy.wait()


def forward_kernel(where, p0, p1, p2, p3, m01, m23, kept_x, kept_y, given_x, given_y, prop, meson, turned, ahead, total):
    order, width = prop.shape[1], p0.shape[-1]
    half = order // 2
    for place, p in enumerate((p0, p1, p2, p3)):
        columns = block(where[place], width)
        prop[:order, columns], prop[order:, columns] = p[0], p[1]
    for n in range(2):
        for place, m in ((4 + n, m01), (6 + n, m23)):
            real, imag = block(where[place], width), block(where[place] + 4, width)
            meson[:, real], meson[:, imag] = m[n, 0], -m[n, 1]
            turned[:, real], turned[:, imag] = m[n, 1], m[n, 0]
    real, imag = dot(meson[...], prop[...], NN), dot(turned[...], prop[...], NN)
    ahead[0, :half], ahead[0, half:order] = real[:half].astype(BF16), (-real[half:]).astype(BF16)
    ahead[0, order : order + half], ahead[0, order + half :] = imag[:half].astype(BF16), (-imag[half:]).astype(BF16)
    ahead[1, :order], ahead[1, order:] = ahead[0, order:], -ahead[0, :order]
    for part in range(2):
        value = dot(prop[...], ahead[part], TN)
        total[part, :half] = value[:half]
        total[part, half:] = -value[half:]
    for n, out in enumerate((kept_x, kept_y, given_x, given_y)):
        out[...] = total[:, :, block(where[8 + n], width)]


def second_kernel(pair, out):
    out[...] = pair[0]


def join_kernel(a, pair, out):
    out[...] = (a[...] + pair[0].astype(F32)).astype(BF16)


def in_rows(kernel, cost, *arrays):
    _, parts, order, width = arrays[-1].shape
    whole = pl.BlockSpec((parts, order, width), lambda i: (0, 0, 0))
    pair = pl.BlockSpec((1, parts, order, width), lambda i: (1, 0, 0, 0))
    return pl.pallas_call(
        kernel,
        grid=(1,),
        out_shape=jax.ShapeDtypeStruct((parts, order, width), BF16),
        in_specs=[whole] * (len(arrays) - 1) + [pair],
        out_specs=whole,
        cost_estimate=pl.CostEstimate(flops=cost, bytes_accessed=1, transcendentals=0),
        name=kernel.__name__,
    )(*arrays)


def shards(near_prop, far_prop, meson):
    _, parts, order, width = meson.shape
    peers = lax.axis_size("tm")
    cols = lax.axis_size("col")
    steps = (peers // 8, 3 * peers // 8)
    j, q = lax.axis_index("tm"), lax.axis_index("col")
    c, k = q >> 1, q & 1

    def level(row):
        return (row >= peers // 2) * 1

    def to_rows(sign, crossed):
        pairs = []
        for row in range(peers):
            for chip in range(2):
                for core in range(2):
                    target = core ^ crossed if sign < 0 else core
                    there = (row + sign * steps[target]) % peers
                    chip_there = chip ^ level(row) ^ level(there)
                    pairs.append((row * cols + 2 * chip + core, there * cols + 2 * chip_there + (core ^ crossed)))
        return pairs

    def in_row(array, by):
        return lax.ppermute(array, "col", [(i, i ^ by) for i in range(cols)])

    def out_of_row(array, sign, crossed):
        return lax.ppermute(array, ("tm", "col"), to_rows(sign, crossed))

    ours = c ^ level(j)
    theirs = 1 - ours

    def pick(array, at):
        return lax.dynamic_index_in_dim(array, at, 0, keepdims=False)

    def prop_at(near_core, at):
        return jnp.where(k == near_core, pick(near_prop, at), pick(far_prop, at))

    m_ours, m_theirs = pick(meson, ours), pick(meson, theirs)
    p_ours, p_sib = prop_at(0, ours), prop_at(1, ours)

    p_from_sib, m_sib = in_row(jnp.stack([p_sib, m_ours]), 1)
    next_1 = out_of_row(jnp.stack([m_ours, m_sib]), -1, 0)
    m_cross = in_row(m_theirs, 2)
    m_last = in_row(m_cross, 1)
    next_2 = out_of_row(jnp.stack([m_cross, m_last]), -1, 0)
    p_cross = in_row(jnp.stack([prop_at(0, theirs), prop_at(1, theirs)]), 2)
    p_cross, next_1 = lax.optimization_barrier((p_cross, next_1))
    p_last = in_row(p_cross[1], 1)

    props = (p_ours, p_from_sib, p_cross[0], p_last)
    mesons = (m_ours, m_sib, m_cross, m_last)
    step = jnp.where(k == 0, steps[0], steps[1])
    to_chip = ours ^ level((j + step) & (peers - 1))
    x, y = 2 * (1 - to_chip), 2 * to_chip
    where_back = jnp.stack([q, q ^ 1, q ^ 2, q ^ 3, x + k, x + 1 - k, y + k, y + 1 - k]).astype(jnp.int32)
    piece = jax.ShapeDtypeStruct((2, parts, order, width), BF16)
    whole = pltpu.VMEM((parts, order, order), BF16)
    wide = pltpu.VMEM((order, 2 * order), BF16)
    vmem, smem = pl.BlockSpec(memory_space=pltpu.VMEM), pl.BlockSpec(memory_space=pltpu.SMEM)
    product = 8 * order**3
    x_out, y_out = pl.pallas_call(
        backward_kernel,
        out_shape=[piece] * 2,
        in_specs=[smem] + [vmem] * 8,
        out_specs=[pl.BlockSpec(memory_space=pltpu.HBM)] * 2,
        scratch_shapes=[wide] * 3 + [pltpu.VMEM((parts, 2 * order, order), BF16), whole, pltpu.SemaphoreType.DMA((2, 4))],
        compiler_params=pltpu.CompilerParams(vmem_limit_bytes=24 * 2**20),
        cost_estimate=pl.CostEstimate(flops=1, bytes_accessed=1, transcendentals=0),
        name="backward",
    )(where_back, *props, *mesons)
    x_in, y_in = out_of_row(x_out, 1, 0), out_of_row(y_out, 1, 0)
    *late, x_out, y_out = lax.optimization_barrier((*props, x_out, y_out))

    u, v = 2 * to_chip, 2 * (1 - to_chip)
    z, w = 2 * (1 - c), 2 * c
    where_next = jnp.stack(
        [q, q ^ 1, q ^ 2, q ^ 3, u + k, u + 1 - k, v + k, v + 1 - k, z + k, w + k, z + 1 - k, w + 1 - k]
    ).astype(jnp.int32)
    kept_x, kept_y, given_x, given_y = pl.pallas_call(
        forward_kernel,
        out_shape=[jax.ShapeDtypeStruct((parts, order, width), F32)] * 4,
        in_specs=[smem] + [vmem] * 6,
        out_specs=[vmem] * 4,
        scratch_shapes=[
            pltpu.VMEM((2 * order, order), BF16),
            wide,
            wide,
            pltpu.VMEM((parts, 2 * order, order), BF16),
            pltpu.VMEM((parts, order, order), F32),
        ],
        compiler_params=pltpu.CompilerParams(vmem_limit_bytes=24 * 2**20),
        cost_estimate=pl.CostEstimate(flops=5 * product, bytes_accessed=14 * parts * order * width * 2, transcendentals=0),
        name="forward",
    )(where_next, *late, next_1, next_2)

    from_sib = in_row((given_x + x_in[1].astype(F32)).astype(BF16), 1)
    sent = kept_x + x_in[0].astype(F32) + from_sib.astype(F32)
    sent = sent.astype(BF16)
    y_in, held = lax.optimization_barrier((y_in, sent))
    from_partner = in_row(sent, 2)
    from_sib_y = in_row(in_rows(join_kernel, 1, given_y, y_in), 1)
    stay = kept_y + y_in[0].astype(F32)
    stay, from_partner, from_sib_y = lax.optimization_barrier((stay, from_partner, from_sib_y))
    slot = lax.broadcasted_iota(jnp.int32, (2, parts, order, width), 0)
    return jnp.where(slot == ours, (stay + from_sib_y.astype(F32))[None], from_partner.astype(F32)[None])


def solution(mesh):
    placed = (P("tm", None, None, "col"), P("tm", None, None, "col"), P("tm", None, None, "col"))
    return jax.shard_map(
        shards, mesh=mesh, in_specs=placed, out_specs=P("tm", None, None, "col"), check_vma=False
    )
```

```python
import jax
import jax.numpy as jnp
from jax import lax
from jax.experimental import pallas as pl
from jax.experimental.pallas import tpu as pltpu
from jax.sharding import PartitionSpec as P


BF16, F32 = jnp.bfloat16, jnp.float32
NT = (((1,), (1,)), ((), ()))
NN = (((1,), (0,)), ((), ()))
TN = (((0,), (0,)), ((), ()))


def dot(a, b, dims):
    return lax.dot_general(a, b, dims, preferred_element_type=F32)


def block(at, width):
    return pl.ds(pl.multiple_of(at * width, width), width)


def backward_kernel(where, p0, p1, p2, p3, m0, m1, m2, m3, x, y, prop, meson, inner, back, sems):
    width = p0.shape[-1]
    half = prop.shape[-1] // 2
    for place, (p, m) in enumerate(((p0, m0), (p1, m1), (p2, m2), (p3, m3))):
        at = where[place]
        sign = jnp.where(at < 2, 1.0, -1.0).astype(F32)
        prop[:, :, block(at, width)] = p[...]
        meson[:, :, block(at, width)] = (m[...].astype(F32) * sign).astype(BF16)
    pr, pi, mr, mi = prop[0], prop[1], meson[0], meson[1]
    inner[0] = (dot(mr, pr, NT) + dot(mi, pi, NT)).astype(BF16)
    inner[1] = (dot(mi, pr, NT) - dot(mr, pi, NT)).astype(BF16)
    ir, ii = inner[0], inner[1]
    copies = []
    for part in range(2):
        total = dot(pr, ii, NN) + dot(pi, ir, NN) if part else dot(pr, ir, NN) - dot(pi, ii, NN)
        back[part, :, :half] = total[:, :half].astype(BF16)
        back[part, :, half:] = (-total[:, half:]).astype(BF16)
        for place, out in enumerate((x.at[0], x.at[1], y.at[0], y.at[1])):
            columns = block(where[4 + place], width)
            copies.append(pltpu.make_async_copy(back.at[part, :, columns], out.at[part], sems.at[part, place]))
            copies[-1].start()
    for copy in copies:
        copy.wait()


def forward_kernel(where, p0, p1, p2, p3, m0, m123, kept_x, kept_y, given_x, given_y, prop, meson, ahead, total):
    width = p0.shape[-1]
    half = prop.shape[-1] // 2
    for place, p in enumerate((p0, p1, p2, p3)):
        prop[:, :, block(where[place], width)] = p[...]
    meson[:, :, block(where[4], width)] = m0[...]
    for n in range(3):
        meson[:, :, block(where[5 + n], width)] = m123[n]
    pr, pi, mr, mi = prop[0], prop[1], meson[0], meson[1]
    for part, value in ((0, dot(mr, pr, NN) - dot(mi, pi, NN)), (1, dot(mr, pi, NN) + dot(mi, pr, NN))):
        ahead[part, :half] = value[:half].astype(BF16)
        ahead[part, half:] = -value[half:].astype(BF16)
    ar, ai = ahead[0], ahead[1]
    for part, value in ((0, dot(pr, ar, TN) + dot(pi, ai, TN)), (1, dot(pr, ai, TN) - dot(pi, ar, TN))):
        total[part, :half] = value[:half]
        total[part, half:] = -value[half:]
    for n, out in enumerate((kept_x, kept_y, given_x, given_y)):
        out[...] = total[:, :, block(where[8 + n], width)]


def second_kernel(pair, out):
    out[...] = pair[0]


def join_kernel(a, pair, out):
    out[...] = (a[...] + pair[0].astype(F32)).astype(BF16)


def in_rows(kernel, cost, *arrays):
    _, parts, order, width = arrays[-1].shape
    whole = pl.BlockSpec((parts, order, width), lambda i: (0, 0, 0))
    pair = pl.BlockSpec((1, parts, order, width), lambda i: (1, 0, 0, 0))
    return pl.pallas_call(
        kernel,
        grid=(1,),
        out_shape=jax.ShapeDtypeStruct((parts, order, width), BF16),
        in_specs=[whole] * (len(arrays) - 1) + [pair],
        out_specs=whole,
        cost_estimate=pl.CostEstimate(flops=cost, bytes_accessed=1, transcendentals=0),
        name=kernel.__name__,
    )(*arrays)


def shards(near_prop, far_prop, meson):
    _, parts, order, width = meson.shape
    peers = lax.axis_size("tm")
    cols = lax.axis_size("col")
    steps = (peers // 8, 3 * peers // 8)
    j, q = lax.axis_index("tm"), lax.axis_index("col")
    c, k = q >> 1, q & 1

    def level(row):
        return (row >= peers // 2) * 1

    def to_rows(sign, crossed):
        pairs = []
        for row in range(peers):
            for chip in range(2):
                for core in range(2):
                    target = core ^ crossed if sign < 0 else core
                    there = (row + sign * steps[target]) % peers
                    chip_there = chip ^ level(row) ^ level(there)
                    pairs.append((row * cols + 2 * chip + core, there * cols + 2 * chip_there + (core ^ crossed)))
        return pairs

    def in_row(array, by):
        return lax.ppermute(array, "col", [(i, i ^ by) for i in range(cols)])

    def out_of_row(array, sign, crossed):
        return lax.ppermute(array, ("tm", "col"), to_rows(sign, crossed))

    ours = c ^ level(j)
    theirs = 1 - ours

    def pick(array, at):
        return lax.dynamic_index_in_dim(array, at, 0, keepdims=False)

    def prop_at(near_core, at):
        return jnp.where(k == near_core, pick(near_prop, at), pick(far_prop, at))

    m_ours, m_theirs = pick(meson, ours), pick(meson, theirs)
    p_ours, p_sib = prop_at(0, ours), prop_at(1, ours)

    p_from_sib, m_sib = in_row(jnp.stack([p_sib, m_ours]), 1)
    next_1 = out_of_row(m_ours, -1, 0)
    m_cross = in_row(m_theirs, 2)
    m_last = in_row(m_cross, 1)
    next_2 = out_of_row(jnp.stack([m_sib, m_cross, m_last]), -1, 0)
    p_cross = in_row(jnp.stack([prop_at(0, theirs), prop_at(1, theirs)]), 2)
    p_cross, next_1 = lax.optimization_barrier((p_cross, next_1))
    p_last = in_row(p_cross[1], 1)

    props = (p_ours, p_from_sib, p_cross[0], p_last)
    mesons = (m_ours, m_sib, m_cross, m_last)
    step = jnp.where(k == 0, steps[0], steps[1])
    to_chip = ours ^ level((j + step) & (peers - 1))
    x, y = 2 * (1 - to_chip), 2 * to_chip
    where_back = jnp.stack([q, q ^ 1, q ^ 2, q ^ 3, x + k, x + 1 - k, y + k, y + 1 - k]).astype(jnp.int32)
    piece = jax.ShapeDtypeStruct((2, parts, order, width), BF16)
    whole = pltpu.VMEM((parts, order, order), BF16)
    vmem, smem = pl.BlockSpec(memory_space=pltpu.VMEM), pl.BlockSpec(memory_space=pltpu.SMEM)
    product = 8 * order**3
    x_out, y_out = pl.pallas_call(
        backward_kernel,
        out_shape=[piece] * 2,
        in_specs=[smem] + [vmem] * 8,
        out_specs=[pl.BlockSpec(memory_space=pltpu.HBM)] * 2,
        scratch_shapes=[whole] * 4 + [pltpu.SemaphoreType.DMA((2, 4))],
        compiler_params=pltpu.CompilerParams(vmem_limit_bytes=24 * 2**20),
        cost_estimate=pl.CostEstimate(flops=1, bytes_accessed=1, transcendentals=0),
        name="backward",
    )(where_back, *props, *mesons)
    x_in, y_in = out_of_row(x_out, 1, 0), out_of_row(y_out, 1, 0)
    *late, x_out, y_out = lax.optimization_barrier((*props, x_out, y_out))

    u, v = 2 * to_chip, 2 * (1 - to_chip)
    z, w = 2 * (1 - c), 2 * c
    where_next = jnp.stack(
        [q, q ^ 1, q ^ 2, q ^ 3, u + k, u + 1 - k, v + k, v + 1 - k, z + k, w + k, z + 1 - k, w + 1 - k]
    ).astype(jnp.int32)
    kept_x, kept_y, given_x, given_y = pl.pallas_call(
        forward_kernel,
        out_shape=[jax.ShapeDtypeStruct((parts, order, width), F32)] * 4,
        in_specs=[smem] + [vmem] * 6,
        out_specs=[vmem] * 4,
        scratch_shapes=[whole] * 3 + [pltpu.VMEM((parts, order, order), F32)],
        compiler_params=pltpu.CompilerParams(vmem_limit_bytes=24 * 2**20),
        cost_estimate=pl.CostEstimate(flops=5 * product, bytes_accessed=14 * parts * order * width * 2, transcendentals=0),
        name="forward",
    )(where_next, *late, next_1, next_2)

    from_sib = in_row((given_x + x_in[1].astype(F32)).astype(BF16), 1)
    sent = kept_x + x_in[0].astype(F32) + from_sib.astype(F32)
    sent = sent.astype(BF16)
    y_in, held = lax.optimization_barrier((y_in, sent))
    from_partner = in_row(sent, 2)
    from_sib_y = in_row(in_rows(join_kernel, 1, given_y, y_in), 1)
    stay = kept_y + y_in[0].astype(F32)
    stay, from_partner, from_sib_y = lax.optimization_barrier((stay, from_partner, from_sib_y))
    slot = lax.broadcasted_iota(jnp.int32, (2, parts, order, width), 0)
    return jnp.where(slot == ours, (stay + from_sib_y.astype(F32))[None], from_partner.astype(F32)[None])


def solution(mesh):
    placed = (P("tm", None, None, "col"), P("tm", None, None, "col"), P("tm", None, None, "col"))
    return jax.shard_map(
        shards, mesh=mesh, in_specs=placed, out_specs=P("tm", None, None, "col"), check_vma=False
    )
```

```python
import jax
import jax.numpy as jnp
from jax import lax
from jax.experimental import pallas as pl
from jax.experimental.pallas import tpu as pltpu
from jax.sharding import PartitionSpec as P


BF16, F32 = jnp.bfloat16, jnp.float32
NT = (((1,), (1,)), ((), ()))
NN = (((1,), (0,)), ((), ()))
TN = (((0,), (0,)), ((), ()))


def dot(a, b, dims):
    return lax.dot_general(a, b, dims, preferred_element_type=F32)


def block(at, width):
    return pl.ds(pl.multiple_of(at * width, width), width)


def backward_kernel(where, p0, p1, p2, p3, m0, m1, m2, m3, x, y, prop, meson, inner, back, sems):
    width = p0.shape[-1]
    half = prop.shape[-1] // 2
    for place, (p, m) in enumerate(((p0, m0), (p1, m1), (p2, m2), (p3, m3))):
        at = where[place]
        sign = jnp.where(at < 2, 1.0, -1.0).astype(F32)
        prop[:, :, block(at, width)] = p[...]
        meson[:, :, block(at, width)] = (m[...].astype(F32) * sign).astype(BF16)
    pr, pi, mr, mi = prop[0], prop[1], meson[0], meson[1]
    inner[0] = (dot(mr, pr, NT) + dot(mi, pi, NT)).astype(BF16)
    inner[1] = (dot(mi, pr, NT) - dot(mr, pi, NT)).astype(BF16)
    ir, ii = inner[0], inner[1]
    copies = []
    for part in range(2):
        total = dot(pr, ii, NN) + dot(pi, ir, NN) if part else dot(pr, ir, NN) - dot(pi, ii, NN)
        back[part, :, :half] = total[:, :half].astype(BF16)
        back[part, :, half:] = (-total[:, half:]).astype(BF16)
        for place, out in enumerate((x.at[0], x.at[1], y.at[0], y.at[1])):
            columns = block(where[4 + place], width)
            copies.append(pltpu.make_async_copy(back.at[part, :, columns], out.at[part], sems.at[part, place]))
            copies[-1].start()
    for copy in copies:
        copy.wait()


def forward_kernel(where, p0, p1, p2, p3, m0, m1, m23, kept_x, kept_y, given_x, given_y, prop, meson, ahead, total):
    width = p0.shape[-1]
    half = prop.shape[-1] // 2
    for place, p in enumerate((p0, p1, p2, p3)):
        prop[:, :, block(where[place], width)] = p[...]
    for n, m in enumerate((m0, m1)):
        meson[:, :, block(where[4 + n], width)] = m[...]
    for n in range(2):
        meson[:, :, block(where[6 + n], width)] = m23[n]
    pr, pi, mr, mi = prop[0], prop[1], meson[0], meson[1]
    for part, value in ((0, dot(mr, pr, NN) - dot(mi, pi, NN)), (1, dot(mr, pi, NN) + dot(mi, pr, NN))):
        ahead[part, :half] = value[:half].astype(BF16)
        ahead[part, half:] = -value[half:].astype(BF16)
    ar, ai = ahead[0], ahead[1]
    for part, value in ((0, dot(pr, ar, TN) + dot(pi, ai, TN)), (1, dot(pr, ai, TN) - dot(pi, ar, TN))):
        total[part, :half] = value[:half]
        total[part, half:] = -value[half:]
    for n, out in enumerate((kept_x, kept_y, given_x, given_y)):
        out[...] = total[:, :, block(where[8 + n], width)].astype(out.dtype)


def second_kernel(pair, out):
    out[...] = pair[0]


def second(pair, cost):
    _, parts, order, width = pair.shape
    return pl.pallas_call(
        second_kernel,
        grid=(1,),
        out_shape=jax.ShapeDtypeStruct((parts, order, width), pair.dtype),
        in_specs=[pl.BlockSpec((1, parts, order, width), lambda i: (1, 0, 0, 0))],
        out_specs=pl.BlockSpec((parts, order, width), lambda i: (0, 0, 0)),
        cost_estimate=pl.CostEstimate(flops=cost, bytes_accessed=1, transcendentals=0),
        name="second",
    )(pair)


def shards(near_prop, far_prop, meson):
    _, parts, order, width = meson.shape
    peers = lax.axis_size("tm")
    cols = lax.axis_size("col")
    steps = (peers // 8, 3 * peers // 8)
    j, q = lax.axis_index("tm"), lax.axis_index("col")
    c, k = q >> 1, q & 1

    def level(row):
        return (row >= peers // 2) * 1

    def to_rows(sign, crossed):
        pairs = []
        for row in range(peers):
            for chip in range(2):
                for core in range(2):
                    target = core ^ crossed if sign < 0 else core
                    there = (row + sign * steps[target]) % peers
                    chip_there = chip ^ level(row) ^ level(there)
                    pairs.append((row * cols + 2 * chip + core, there * cols + 2 * chip_there + (core ^ crossed)))
        return pairs

    def in_row(array, by):
        return lax.ppermute(array, "col", [(i, i ^ by) for i in range(cols)])

    def out_of_row(array, sign, crossed):
        return lax.ppermute(array, ("tm", "col"), to_rows(sign, crossed))

    ours = c ^ level(j)
    theirs = 1 - ours

    def pick(array, at):
        return lax.dynamic_index_in_dim(array, at, 0, keepdims=False)

    def prop_at(near_core, at):
        return jnp.where(k == near_core, pick(near_prop, at), pick(far_prop, at))

    m_ours, m_theirs = pick(meson, ours), pick(meson, theirs)
    p_ours, p_sib = prop_at(0, ours), prop_at(1, ours)

    p_from_sib, m_sib = in_row(jnp.stack([p_sib, m_ours]), 1)
    next_1, next_b = out_of_row(m_ours, -1, 0), out_of_row(m_ours, -1, 1)
    m_cross = in_row(m_theirs, 2)
    m_cross, next_1 = lax.optimization_barrier((m_cross, next_1))
    m_last = in_row(m_cross, 1)
    next_2 = out_of_row(jnp.stack([m_cross, m_last]), -1, 0)
    p_cross = in_row(jnp.stack([prop_at(0, theirs), prop_at(1, theirs)]), 2)
    p_cross, next_b = lax.optimization_barrier((p_cross, next_b))
    p_last = in_row(p_cross[1], 1)

    props = (p_ours, p_from_sib, p_cross[0], p_last)
    mesons = (m_ours, m_sib, m_cross, m_last)
    step = jnp.where(k == 0, steps[0], steps[1])
    to_chip = ours ^ level((j + step) & (peers - 1))
    x, y = 2 * (1 - to_chip), 2 * to_chip
    where_back = jnp.stack([q, q ^ 1, q ^ 2, q ^ 3, x + k, x + 1 - k, y + k, y + 1 - k]).astype(jnp.int32)
    piece = jax.ShapeDtypeStruct((2, parts, order, width), BF16)
    whole = pltpu.VMEM((parts, order, order), BF16)
    vmem, smem = pl.BlockSpec(memory_space=pltpu.VMEM), pl.BlockSpec(memory_space=pltpu.SMEM)
    product = 8 * order**3
    x_out, y_out = pl.pallas_call(
        backward_kernel,
        out_shape=[piece] * 2,
        in_specs=[smem] + [vmem] * 8,
        out_specs=[pl.BlockSpec(memory_space=pltpu.HBM)] * 2,
        scratch_shapes=[whole] * 4 + [pltpu.SemaphoreType.DMA((2, 4))],
        compiler_params=pltpu.CompilerParams(vmem_limit_bytes=24 * 2**20),
        cost_estimate=pl.CostEstimate(flops=1, bytes_accessed=1, transcendentals=0),
        name="backward",
    )(where_back, *props, *mesons)
    x_in, y_in = out_of_row(x_out, 1, 0), out_of_row(y_out, 1, 0)
    *late, x_out, y_out = lax.optimization_barrier((*props, x_out, y_out))

    u, v = 2 * to_chip, 2 * (1 - to_chip)
    z, w = 2 * (1 - c), 2 * c
    where_next = jnp.stack(
        [q, q ^ 1, q ^ 2, q ^ 3, u + k, u + 1 - k, v + k, v + 1 - k, z + k, w + k, z + 1 - k, w + 1 - k]
    ).astype(jnp.int32)
    kept_x, kept_y, given_x, given_y = pl.pallas_call(
        forward_kernel,
        out_shape=[jax.ShapeDtypeStruct((parts, order, width), d) for d in (F32, F32, F32, BF16)],
        in_specs=[smem] + [vmem] * 7,
        out_specs=[vmem] * 4,
        scratch_shapes=[whole] * 3 + [pltpu.VMEM((parts, order, order), F32)],
        compiler_params=pltpu.CompilerParams(vmem_limit_bytes=24 * 2**20),
        cost_estimate=pl.CostEstimate(flops=int(3 * product), bytes_accessed=14 * parts * order * width * 2, transcendentals=0),
        name="forward",
    )(where_next, *late, next_1, next_b, next_2)

    passed = in_row(given_y, 1)
    from_sib = in_row((given_x + x_in[1].astype(F32)).astype(BF16), 1)
    sent = (kept_x + x_in[0].astype(F32) + from_sib.astype(F32)).astype(BF16)
    from_partner = in_row(sent, 2)
    y_in, held = lax.optimization_barrier((y_in, sent))
    y_sib = in_row(second(y_in, 1), 1)
    stay = kept_y + passed.astype(F32) + y_in[0].astype(F32)
    stay, from_partner, y_sib = lax.optimization_barrier((stay, from_partner, y_sib))
    slot = lax.broadcasted_iota(jnp.int32, (2, parts, order, width), 0)
    return jnp.where(slot == ours, (stay + y_sib.astype(F32))[None], from_partner.astype(F32)[None])


def solution(mesh):
    placed = (P("tm", None, None, "col"), P("tm", None, None, "col"), P("tm", None, None, "col"))
    return jax.shard_map(
        shards, mesh=mesh, in_specs=placed, out_specs=P("tm", None, None, "col"), check_vma=False
    )
```

```python
import jax
import jax.numpy as jnp
from jax import lax
from jax.experimental import pallas as pl
from jax.experimental.pallas import tpu as pltpu
from jax.sharding import PartitionSpec as P


BF16, F32 = jnp.bfloat16, jnp.float32
NT = (((1,), (1,)), ((), ()))
NN = (((1,), (0,)), ((), ()))
TN = (((0,), (0,)), ((), ()))


def dot(a, b, dims):
    return lax.dot_general(a, b, dims, preferred_element_type=F32)


def block(at, width):
    return pl.ds(pl.multiple_of(at * width, width), width)


def backward_kernel(where, p0, p1, p2, p3, m0, m1, m2, m3, x, y, prop, meson, inner, back, sems):
    width = p0.shape[-1]
    half = prop.shape[-1] // 2
    for place, (p, m) in enumerate(((p0, m0), (p1, m1), (p2, m2), (p3, m3))):
        at = where[place]
        sign = jnp.where(at < 2, 1.0, -1.0).astype(F32)
        prop[:, :, block(at, width)] = p[...]
        meson[:, :, block(at, width)] = (m[...].astype(F32) * sign).astype(BF16)
    pr, pi, mr, mi = prop[0], prop[1], meson[0], meson[1]
    inner[0] = (dot(mr, pr, NT) + dot(mi, pi, NT)).astype(BF16)
    inner[1] = (dot(mi, pr, NT) - dot(mr, pi, NT)).astype(BF16)
    ir, ii = inner[0], inner[1]
    copies = []
    for part in range(2):
        total = dot(pr, ii, NN) + dot(pi, ir, NN) if part else dot(pr, ir, NN) - dot(pi, ii, NN)
        back[part, :, :half] = total[:, :half].astype(BF16)
        back[part, :, half:] = (-total[:, half:]).astype(BF16)
        for place, out in enumerate((x.at[0], x.at[1], y.at[0], y.at[1])):
            columns = block(where[4 + place], width)
            copies.append(pltpu.make_async_copy(back.at[part, :, columns], out.at[part], sems.at[part, place]))
            copies[-1].start()
    for copy in copies:
        copy.wait()


def forward_kernel(where, p0, p1, p2, p3, m0, m123, kept_x, kept_y, given_x, given_y, prop, meson, ahead, total):
    width = p0.shape[-1]
    half = prop.shape[-1] // 2
    for place, p in enumerate((p0, p1, p2, p3)):
        prop[:, :, block(where[place], width)] = p[...]
    meson[:, :, block(where[4], width)] = m0[...]
    for n in range(3):
        meson[:, :, block(where[5 + n], width)] = m123[n]
    pr, pi, mr, mi = prop[0], prop[1], meson[0], meson[1]
    for part, value in ((0, dot(mr, pr, NN) - dot(mi, pi, NN)), (1, dot(mr, pi, NN) + dot(mi, pr, NN))):
        ahead[part, :half] = value[:half].astype(BF16)
        ahead[part, half:] = -value[half:].astype(BF16)
    ar, ai = ahead[0], ahead[1]
    for part, value in ((0, dot(pr, ar, TN) + dot(pi, ai, TN)), (1, dot(pr, ai, TN) - dot(pi, ar, TN))):
        total[part, :half] = value[:half]
        total[part, half:] = -value[half:]
    for n, out in enumerate((kept_x, kept_y, given_x, given_y)):
        out[...] = total[:, :, block(where[8 + n], width)].astype(out.dtype)


def second_kernel(pair, out):
    out[...] = pair[0]


def second(pair, cost):
    _, parts, order, width = pair.shape
    return pl.pallas_call(
        second_kernel,
        grid=(1,),
        out_shape=jax.ShapeDtypeStruct((parts, order, width), pair.dtype),
        in_specs=[pl.BlockSpec((1, parts, order, width), lambda i: (1, 0, 0, 0))],
        out_specs=pl.BlockSpec((parts, order, width), lambda i: (0, 0, 0)),
        cost_estimate=pl.CostEstimate(flops=cost, bytes_accessed=1, transcendentals=0),
        name="second",
    )(pair)


def shards(near_prop, far_prop, meson):
    _, parts, order, width = meson.shape
    peers = lax.axis_size("tm")
    cols = lax.axis_size("col")
    steps = (peers // 8, 3 * peers // 8)
    j, q = lax.axis_index("tm"), lax.axis_index("col")
    c, k = q >> 1, q & 1

    def level(row):
        return (row >= peers // 2) * 1

    def to_rows(sign, crossed):
        pairs = []
        for row in range(peers):
            for chip in range(2):
                for core in range(2):
                    target = core ^ crossed if sign < 0 else core
                    there = (row + sign * steps[target]) % peers
                    chip_there = chip ^ level(row) ^ level(there)
                    pairs.append((row * cols + 2 * chip + core, there * cols + 2 * chip_there + (core ^ crossed)))
        return pairs

    def in_row(array, by):
        return lax.ppermute(array, "col", [(i, i ^ by) for i in range(cols)])

    def out_of_row(array, sign, crossed):
        return lax.ppermute(array, ("tm", "col"), to_rows(sign, crossed))

    ours = c ^ level(j)
    theirs = 1 - ours

    def pick(array, at):
        return lax.dynamic_index_in_dim(array, at, 0, keepdims=False)

    def prop_at(near_core, at):
        return jnp.where(k == near_core, pick(near_prop, at), pick(far_prop, at))

    m_ours, m_theirs = pick(meson, ours), pick(meson, theirs)
    p_ours, p_sib = prop_at(0, ours), prop_at(1, ours)

    p_from_sib, m_sib = in_row(jnp.stack([p_sib, m_ours]), 1)
    next_1 = out_of_row(m_ours, -1, 0)
    m_cross = in_row(m_theirs, 2)
    m_cross, next_1 = lax.optimization_barrier((m_cross, next_1))
    m_last = in_row(m_cross, 1)
    next_2 = out_of_row(jnp.stack([m_sib, m_cross, m_last]), -1, 0)
    p_cross = in_row(jnp.stack([prop_at(0, theirs), prop_at(1, theirs)]), 2)
    p_last = in_row(p_cross[1], 1)

    props = (p_ours, p_from_sib, p_cross[0], p_last)
    mesons = (m_ours, m_sib, m_cross, m_last)
    step = jnp.where(k == 0, steps[0], steps[1])
    to_chip = ours ^ level((j + step) & (peers - 1))
    x, y = 2 * (1 - to_chip), 2 * to_chip
    where_back = jnp.stack([q, q ^ 1, q ^ 2, q ^ 3, x + k, x + 1 - k, y + k, y + 1 - k]).astype(jnp.int32)
    piece = jax.ShapeDtypeStruct((2, parts, order, width), BF16)
    whole = pltpu.VMEM((parts, order, order), BF16)
    vmem, smem = pl.BlockSpec(memory_space=pltpu.VMEM), pl.BlockSpec(memory_space=pltpu.SMEM)
    product = 8 * order**3
    x_out, y_out = pl.pallas_call(
        backward_kernel,
        out_shape=[piece] * 2,
        in_specs=[smem] + [vmem] * 8,
        out_specs=[pl.BlockSpec(memory_space=pltpu.HBM)] * 2,
        scratch_shapes=[whole] * 4 + [pltpu.SemaphoreType.DMA((2, 4))],
        compiler_params=pltpu.CompilerParams(vmem_limit_bytes=24 * 2**20),
        cost_estimate=pl.CostEstimate(flops=1, bytes_accessed=1, transcendentals=0),
        name="backward",
    )(where_back, *props, *mesons)
    x_in, y_in = out_of_row(x_out, 1, 0), out_of_row(y_out, 1, 0)
    *late, x_out, y_out = lax.optimization_barrier((*props, x_out, y_out))

    u, v = 2 * to_chip, 2 * (1 - to_chip)
    z, w = 2 * (1 - c), 2 * c
    where_next = jnp.stack(
        [q, q ^ 1, q ^ 2, q ^ 3, u + k, u + 1 - k, v + k, v + 1 - k, z + k, w + k, z + 1 - k, w + 1 - k]
    ).astype(jnp.int32)
    kept_x, kept_y, given_x, given_y = pl.pallas_call(
        forward_kernel,
        out_shape=[jax.ShapeDtypeStruct((parts, order, width), d) for d in (F32, F32, F32, BF16)],
        in_specs=[smem] + [vmem] * 6,
        out_specs=[vmem] * 4,
        scratch_shapes=[whole] * 3 + [pltpu.VMEM((parts, order, order), F32)],
        compiler_params=pltpu.CompilerParams(vmem_limit_bytes=24 * 2**20),
        cost_estimate=pl.CostEstimate(flops=int(3 * product), bytes_accessed=14 * parts * order * width * 2, transcendentals=0),
        name="forward",
    )(where_next, *late, next_1, next_2)

    passed = in_row(given_y, 1)
    from_sib = in_row((given_x + x_in[1].astype(F32)).astype(BF16), 1)
    sent = (kept_x + x_in[0].astype(F32) + from_sib.astype(F32)).astype(BF16)
    from_partner = in_row(sent, 2)
    y_in, held = lax.optimization_barrier((y_in, sent))
    y_sib = in_row(second(y_in, 1), 1)
    stay = kept_y + passed.astype(F32) + y_in[0].astype(F32)
    stay, from_partner, y_sib = lax.optimization_barrier((stay, from_partner, y_sib))
    slot = lax.broadcasted_iota(jnp.int32, (2, parts, order, width), 0)
    return jnp.where(slot == ours, (stay + y_sib.astype(F32))[None], from_partner.astype(F32)[None])


def solution(mesh):
    placed = (P("tm", None, None, "col"), P("tm", None, None, "col"), P("tm", None, None, "col"))
    return jax.shard_map(
        shards, mesh=mesh, in_specs=placed, out_specs=P("tm", None, None, "col"), check_vma=False
    )
```

```python
import jax
import jax.numpy as jnp
from jax import lax
from jax.experimental import pallas as pl
from jax.experimental.pallas import tpu as pltpu
from jax.sharding import PartitionSpec as P


BF16, F32 = jnp.bfloat16, jnp.float32
NT = (((1,), (1,)), ((), ()))
NN = (((1,), (0,)), ((), ()))
TN = (((0,), (0,)), ((), ()))


def dot(a, b, dims):
    return lax.dot_general(a, b, dims, preferred_element_type=F32)


def block(at, width):
    return pl.ds(pl.multiple_of(at * width, width), width)


def backward_kernel(where, p0, p1, p2, p3, m0, m1, m2, m3, x, y, prop, meson, inner, back, sems):
    width = p0.shape[-1]
    half = prop.shape[-1] // 2
    for place, (p, m) in enumerate(((p0, m0), (p1, m1), (p2, m2), (p3, m3))):
        at = where[place]
        sign = jnp.where(at < 2, 1.0, -1.0).astype(F32)
        prop[:, :, block(at, width)] = p[...]
        meson[:, :, block(at, width)] = (m[...].astype(F32) * sign).astype(BF16)
    pr, pi, mr, mi = prop[0], prop[1], meson[0], meson[1]
    inner[0] = (dot(mr, pr, NT) + dot(mi, pi, NT)).astype(BF16)
    inner[1] = (dot(mi, pr, NT) - dot(mr, pi, NT)).astype(BF16)
    ir, ii = inner[0], inner[1]
    copies = []
    for part in range(2):
        total = dot(pr, ii, NN) + dot(pi, ir, NN) if part else dot(pr, ir, NN) - dot(pi, ii, NN)
        back[part, :, :half] = total[:, :half].astype(BF16)
        back[part, :, half:] = (-total[:, half:]).astype(BF16)
        for place, out in enumerate((x.at[0], x.at[1], y.at[0], y.at[1])):
            columns = block(where[4 + place], width)
            copies.append(pltpu.make_async_copy(back.at[part, :, columns], out.at[part], sems.at[part, place]))
            copies[-1].start()
    for copy in copies:
        copy.wait()


def forward_kernel(where, p0, p1, p2, p3, m0, m123, kept_x, kept_y, given_x, given_y, prop, meson, ahead, total):
    width = p0.shape[-1]
    half = prop.shape[-1] // 2
    for place, p in enumerate((p0, p1, p2, p3)):
        prop[:, :, block(where[place], width)] = p[...]
    meson[:, :, block(where[4], width)] = m0[...]
    for n in range(3):
        meson[:, :, block(where[5 + n], width)] = m123[n]
    pr, pi, mr, mi = prop[0], prop[1], meson[0], meson[1]
    for part, value in ((0, dot(mr, pr, NN) - dot(mi, pi, NN)), (1, dot(mr, pi, NN) + dot(mi, pr, NN))):
        ahead[part, :half] = value[:half].astype(BF16)
        ahead[part, half:] = -value[half:].astype(BF16)
    ar, ai = ahead[0], ahead[1]
    for part, value in ((0, dot(pr, ar, TN) + dot(pi, ai, TN)), (1, dot(pr, ai, TN) - dot(pi, ar, TN))):
        total[part, :half] = value[:half]
        total[part, half:] = -value[half:]
    for n, out in enumerate((kept_x, kept_y, given_x, given_y)):
        out[...] = total[:, :, block(where[8 + n], width)].astype(out.dtype)


def second_kernel(pair, out):
    out[...] = pair[0]


def second(pair, cost):
    _, parts, order, width = pair.shape
    return pl.pallas_call(
        second_kernel,
        grid=(1,),
        out_shape=jax.ShapeDtypeStruct((parts, order, width), pair.dtype),
        in_specs=[pl.BlockSpec((1, parts, order, width), lambda i: (1, 0, 0, 0))],
        out_specs=pl.BlockSpec((parts, order, width), lambda i: (0, 0, 0)),
        cost_estimate=pl.CostEstimate(flops=cost, bytes_accessed=1, transcendentals=0),
        name="second",
    )(pair)


def shards(near_prop, far_prop, meson):
    _, parts, order, width = meson.shape
    peers = lax.axis_size("tm")
    cols = lax.axis_size("col")
    steps = (peers // 8, 3 * peers // 8)
    j, q = lax.axis_index("tm"), lax.axis_index("col")
    c, k = q >> 1, q & 1

    def level(row):
        return (row >= peers // 2) * 1

    def to_rows(sign, crossed):
        pairs = []
        for row in range(peers):
            for chip in range(2):
                for core in range(2):
                    target = core ^ crossed if sign < 0 else core
                    there = (row + sign * steps[target]) % peers
                    chip_there = chip ^ level(row) ^ level(there)
                    pairs.append((row * cols + 2 * chip + core, there * cols + 2 * chip_there + (core ^ crossed)))
        return pairs

    def in_row(array, by):
        return lax.ppermute(array, "col", [(i, i ^ by) for i in range(cols)])

    def out_of_row(array, sign, crossed):
        return lax.ppermute(array, ("tm", "col"), to_rows(sign, crossed))

    ours = c ^ level(j)
    theirs = 1 - ours

    def pick(array, at):
        return lax.dynamic_index_in_dim(array, at, 0, keepdims=False)

    def prop_at(near_core, at):
        return jnp.where(k == near_core, pick(near_prop, at), pick(far_prop, at))

    m_ours, m_theirs = pick(meson, ours), pick(meson, theirs)
    p_ours, p_sib = prop_at(0, ours), prop_at(1, ours)

    p_from_sib, m_sib = in_row(jnp.stack([p_sib, m_ours]), 1)
    next_1 = out_of_row(m_ours, -1, 0)
    m_cross = in_row(m_theirs, 2)
    m_last = in_row(m_cross, 1)
    next_2 = out_of_row(jnp.stack([m_sib, m_cross, m_last]), -1, 0)
    p_cross = in_row(jnp.stack([prop_at(0, theirs), prop_at(1, theirs)]), 2)
    p_cross, next_1 = lax.optimization_barrier((p_cross, next_1))
    p_last = in_row(p_cross[1], 1)

    props = (p_ours, p_from_sib, p_cross[0], p_last)
    mesons = (m_ours, m_sib, m_cross, m_last)
    step = jnp.where(k == 0, steps[0], steps[1])
    to_chip = ours ^ level((j + step) & (peers - 1))
    x, y = 2 * (1 - to_chip), 2 * to_chip
    where_back = jnp.stack([q, q ^ 1, q ^ 2, q ^ 3, x + k, x + 1 - k, y + k, y + 1 - k]).astype(jnp.int32)
    piece = jax.ShapeDtypeStruct((2, parts, order, width), BF16)
    whole = pltpu.VMEM((parts, order, order), BF16)
    vmem, smem = pl.BlockSpec(memory_space=pltpu.VMEM), pl.BlockSpec(memory_space=pltpu.SMEM)
    product = 8 * order**3
    x_out, y_out = pl.pallas_call(
        backward_kernel,
        out_shape=[piece] * 2,
        in_specs=[smem] + [vmem] * 8,
        out_specs=[pl.BlockSpec(memory_space=pltpu.HBM)] * 2,
        scratch_shapes=[whole] * 4 + [pltpu.SemaphoreType.DMA((2, 4))],
        compiler_params=pltpu.CompilerParams(vmem_limit_bytes=24 * 2**20),
        cost_estimate=pl.CostEstimate(flops=1, bytes_accessed=1, transcendentals=0),
        name="backward",
    )(where_back, *props, *mesons)
    x_in, y_in = out_of_row(x_out, 1, 0), out_of_row(y_out, 1, 0)
    *late, x_out, y_out = lax.optimization_barrier((*props, x_out, y_out))

    u, v = 2 * to_chip, 2 * (1 - to_chip)
    z, w = 2 * (1 - c), 2 * c
    where_next = jnp.stack(
        [q, q ^ 1, q ^ 2, q ^ 3, u + k, u + 1 - k, v + k, v + 1 - k, z + k, w + k, z + 1 - k, w + 1 - k]
    ).astype(jnp.int32)
    kept_x, kept_y, given_x, given_y = pl.pallas_call(
        forward_kernel,
        out_shape=[jax.ShapeDtypeStruct((parts, order, width), d) for d in (F32, F32, F32, BF16)],
        in_specs=[smem] + [vmem] * 6,
        out_specs=[vmem] * 4,
        scratch_shapes=[whole] * 3 + [pltpu.VMEM((parts, order, order), F32)],
        compiler_params=pltpu.CompilerParams(vmem_limit_bytes=24 * 2**20),
        cost_estimate=pl.CostEstimate(flops=int(3 * product), bytes_accessed=14 * parts * order * width * 2, transcendentals=0),
        name="forward",
    )(where_next, *late, next_1, next_2)

    passed = in_row(given_y, 1)
    from_sib = in_row((given_x + x_in[1].astype(F32)).astype(BF16), 1)
    sent = (kept_x + x_in[0].astype(F32) + from_sib.astype(F32)).astype(BF16)
    from_partner = in_row(sent, 2)
    y_in, held = lax.optimization_barrier((y_in, sent))
    y_sib = in_row(second(y_in, 1), 1)
    stay = kept_y + passed.astype(F32) + y_in[0].astype(F32)
    stay, from_partner, y_sib = lax.optimization_barrier((stay, from_partner, y_sib))
    slot = lax.broadcasted_iota(jnp.int32, (2, parts, order, width), 0)
    return jnp.where(slot == ours, (stay + y_sib.astype(F32))[None], from_partner.astype(F32)[None])


def solution(mesh):
    placed = (P("tm", None, None, "col"), P("tm", None, None, "col"), P("tm", None, None, "col"))
    return jax.shard_map(
        shards, mesh=mesh, in_specs=placed, out_specs=P("tm", None, None, "col"), check_vma=False
    )
```

```python
import jax
import jax.numpy as jnp
from jax import lax
from jax.experimental import pallas as pl
from jax.experimental.pallas import tpu as pltpu
from jax.sharding import PartitionSpec as P


BF16, F32 = jnp.bfloat16, jnp.float32
NT = (((1,), (1,)), ((), ()))
NN = (((1,), (0,)), ((), ()))
TN = (((0,), (0,)), ((), ()))


def dot(a, b, dims):
    return lax.dot_general(a, b, dims, preferred_element_type=F32)


def block(at, width):
    return pl.ds(pl.multiple_of(at * width, width), width)


def backward_kernel(where, p0, p1, p2, p3, m0, m1, m2, m3, x, y, prop, meson, inner, back, sems):
    width = p0.shape[-1]
    half = prop.shape[-1] // 2
    for place, (p, m) in enumerate(((p0, m0), (p1, m1), (p2, m2), (p3, m3))):
        at = where[place]
        sign = jnp.where(at < 2, 1.0, -1.0).astype(F32)
        prop[:, :, block(at, width)] = p[...]
        meson[:, :, block(at, width)] = (m[...].astype(F32) * sign).astype(BF16)
    pr, pi, mr, mi = prop[0], prop[1], meson[0], meson[1]
    inner[0] = (dot(mr, pr, NT) + dot(mi, pi, NT)).astype(BF16)
    inner[1] = (dot(mi, pr, NT) - dot(mr, pi, NT)).astype(BF16)
    ir, ii = inner[0], inner[1]
    copies = []
    for part in range(2):
        total = dot(pr, ii, NN) + dot(pi, ir, NN) if part else dot(pr, ir, NN) - dot(pi, ii, NN)
        back[part, :, :half] = total[:, :half].astype(BF16)
        back[part, :, half:] = (-total[:, half:]).astype(BF16)
        for place, out in enumerate((x.at[0], x.at[1], y.at[0], y.at[1])):
            columns = block(where[4 + place], width)
            copies.append(pltpu.make_async_copy(back.at[part, :, columns], out.at[part], sems.at[part, place]))
            copies[-1].start()
    for copy in copies:
        copy.wait()


def forward_kernel(where, p0, p1, p2, p3, m0, m123, kept_x, kept_y, given_x, given_y, prop, meson, ahead, total):
    width = p0.shape[-1]
    half = prop.shape[-1] // 2
    for place, p in enumerate((p0, p1, p2, p3)):
        prop[:, :, block(where[place], width)] = p[...]
    meson[:, :, block(where[4], width)] = m0[...]
    for n in range(3):
        meson[:, :, block(where[5 + n], width)] = m123[n]
    pr, pi, mr, mi = prop[0], prop[1], meson[0], meson[1]
    for part, value in ((0, dot(mr, pr, NN) - dot(mi, pi, NN)), (1, dot(mr, pi, NN) + dot(mi, pr, NN))):
        ahead[part, :half] = value[:half].astype(BF16)
        ahead[part, half:] = -value[half:].astype(BF16)
    ar, ai = ahead[0], ahead[1]
    for part, value in ((0, dot(pr, ar, TN) + dot(pi, ai, TN)), (1, dot(pr, ai, TN) - dot(pi, ar, TN))):
        total[part, :half] = value[:half]
        total[part, half:] = -value[half:]
    for n, out in enumerate((kept_x, kept_y, given_x, given_y)):
        out[...] = total[:, :, block(where[8 + n], width)]


def second_kernel(pair, out):
    out[...] = pair[0]


def join_kernel(a, pair, out):
    out[...] = (a[...] + pair[0].astype(F32)).astype(BF16)


def in_rows(kernel, cost, *arrays):
    _, parts, order, width = arrays[-1].shape
    whole = pl.BlockSpec((parts, order, width), lambda i: (0, 0, 0))
    pair = pl.BlockSpec((1, parts, order, width), lambda i: (1, 0, 0, 0))
    return pl.pallas_call(
        kernel,
        grid=(1,),
        out_shape=jax.ShapeDtypeStruct((parts, order, width), BF16),
        in_specs=[whole] * (len(arrays) - 1) + [pair],
        out_specs=whole,
        cost_estimate=pl.CostEstimate(flops=cost, bytes_accessed=1, transcendentals=0),
        name=kernel.__name__,
    )(*arrays)


def shards(near_prop, far_prop, meson):
    _, parts, order, width = meson.shape
    peers = lax.axis_size("tm")
    cols = lax.axis_size("col")
    steps = (peers // 8, 3 * peers // 8)
    j, q = lax.axis_index("tm"), lax.axis_index("col")
    c, k = q >> 1, q & 1

    def level(row):
        return (row >= peers // 2) * 1

    def to_rows(sign, crossed):
        pairs = []
        for row in range(peers):
            for chip in range(2):
                for core in range(2):
                    target = core ^ crossed if sign < 0 else core
                    there = (row + sign * steps[target]) % peers
                    chip_there = chip ^ level(row) ^ level(there)
                    pairs.append((row * cols + 2 * chip + core, there * cols + 2 * chip_there + (core ^ crossed)))
        return pairs

    def in_row(array, by):
        return lax.ppermute(array, "col", [(i, i ^ by) for i in range(cols)])

    def out_of_row(array, sign, crossed):
        return lax.ppermute(array, ("tm", "col"), to_rows(sign, crossed))

    ours = c ^ level(j)
    theirs = 1 - ours

    def pick(array, at):
        return lax.dynamic_index_in_dim(array, at, 0, keepdims=False)

    def prop_at(near_core, at):
        return jnp.where(k == near_core, pick(near_prop, at), pick(far_prop, at))

    m_ours, m_theirs = pick(meson, ours), pick(meson, theirs)
    p_ours, p_sib = prop_at(0, ours), prop_at(1, ours)

    p_from_sib, m_sib = in_row(jnp.stack([p_sib, m_ours]), 1)
    next_1 = out_of_row(m_ours, -1, 0)
    m_cross = in_row(m_theirs, 2)
    m_last = in_row(m_cross, 1)
    next_2 = out_of_row(jnp.stack([m_sib, m_cross, m_last]), -1, 0)
    p_cross = in_row(jnp.stack([prop_at(0, theirs), prop_at(1, theirs)]), 2)
    p_cross, next_1 = lax.optimization_barrier((p_cross, next_1))
    p_last = in_row(p_cross[1], 1)

    props = (p_ours, p_from_sib, p_cross[0], p_last)
    mesons = (m_ours, m_sib, m_cross, m_last)
    step = jnp.where(k == 0, steps[0], steps[1])
    to_chip = ours ^ level((j + step) & (peers - 1))
    x, y = 2 * (1 - to_chip), 2 * to_chip
    where_back = jnp.stack([q, q ^ 1, q ^ 2, q ^ 3, x + k, x + 1 - k, y + k, y + 1 - k]).astype(jnp.int32)
    piece = jax.ShapeDtypeStruct((2, parts, order, width), BF16)
    whole = pltpu.VMEM((parts, order, order), BF16)
    vmem, smem = pl.BlockSpec(memory_space=pltpu.VMEM), pl.BlockSpec(memory_space=pltpu.SMEM)
    product = 8 * order**3
    x_out, y_out = pl.pallas_call(
        backward_kernel,
        out_shape=[piece] * 2,
        in_specs=[smem] + [vmem] * 8,
        out_specs=[pl.BlockSpec(memory_space=pltpu.HBM)] * 2,
        scratch_shapes=[whole] * 4 + [pltpu.SemaphoreType.DMA((2, 4))],
        compiler_params=pltpu.CompilerParams(vmem_limit_bytes=24 * 2**20),
        cost_estimate=pl.CostEstimate(flops=1, bytes_accessed=1, transcendentals=0),
        name="backward",
    )(where_back, *props, *mesons)
    x_in, y_in = out_of_row(x_out, 1, 0), out_of_row(y_out, 1, 0)
    *late, x_out, y_out = lax.optimization_barrier((*props, x_out, y_out))

    u, v = 2 * to_chip, 2 * (1 - to_chip)
    z, w = 2 * (1 - c), 2 * c
    where_next = jnp.stack(
        [q, q ^ 1, q ^ 2, q ^ 3, u + k, u + 1 - k, v + k, v + 1 - k, z + k, w + k, z + 1 - k, w + 1 - k]
    ).astype(jnp.int32)
    kept_x, kept_y, given_x, given_y = pl.pallas_call(
        forward_kernel,
        out_shape=[jax.ShapeDtypeStruct((parts, order, width), F32)] * 4,
        in_specs=[smem] + [vmem] * 6,
        out_specs=[vmem] * 4,
        scratch_shapes=[whole] * 3 + [pltpu.VMEM((parts, order, order), F32)],
        compiler_params=pltpu.CompilerParams(vmem_limit_bytes=24 * 2**20),
        cost_estimate=pl.CostEstimate(flops=5 * product, bytes_accessed=14 * parts * order * width * 2, transcendentals=0),
        name="forward",
    )(where_next, *late, next_1, next_2)

    from_sib = in_row((given_x + x_in[1].astype(F32)).astype(BF16), 1)
    sent = kept_x + x_in[0].astype(F32) + from_sib.astype(F32)
    sent = sent.astype(BF16)
    y_now, held = lax.optimization_barrier((y_in, sent))
    from_partner = in_row(sent, 2)
    from_sib_y = in_row((given_y + y_now[1].astype(F32)).astype(BF16), 1)
    stay = kept_y + y_in[0].astype(F32)
    stay, from_partner, from_sib_y = lax.optimization_barrier((stay, from_partner, from_sib_y))
    slot = lax.broadcasted_iota(jnp.int32, (2, parts, order, width), 0)
    return jnp.where(slot == ours, (stay + from_sib_y.astype(F32))[None], from_partner.astype(F32)[None])


def solution(mesh):
    placed = (P("tm", None, None, "col"), P("tm", None, None, "col"), P("tm", None, None, "col"))
    return jax.shard_map(
        shards, mesh=mesh, in_specs=placed, out_specs=P("tm", None, None, "col"), check_vma=False
    )
```

```python
import jax
import jax.numpy as jnp
from jax import lax
from jax.experimental import pallas as pl
from jax.experimental.pallas import tpu as pltpu
from jax.sharding import PartitionSpec as P


BF16, F32 = jnp.bfloat16, jnp.float32
NT = (((1,), (1,)), ((), ()))
NN = (((1,), (0,)), ((), ()))
TN = (((0,), (0,)), ((), ()))


def dot(a, b, dims):
    return lax.dot_general(a, b, dims, preferred_element_type=F32)


def block(at, width):
    return pl.ds(pl.multiple_of(at * width, width), width)


def backward_kernel(where, p0, p1, p2, p3, m0, m1, m2, m3, x, y, prop, meson, inner, back, sems):
    width = p0.shape[-1]
    half = prop.shape[-1] // 2
    for place, (p, m) in enumerate(((p0, m0), (p1, m1), (p2, m2), (p3, m3))):
        at = where[place]
        sign = jnp.where(at < 2, 1.0, -1.0).astype(F32)
        prop[:, :, block(at, width)] = p[...]
        meson[:, :, block(at, width)] = (m[...].astype(F32) * sign).astype(BF16)
    pr, pi, mr, mi = prop[0], prop[1], meson[0], meson[1]
    inner[0] = (dot(mr, pr, NT) + dot(mi, pi, NT)).astype(BF16)
    inner[1] = (dot(mi, pr, NT) - dot(mr, pi, NT)).astype(BF16)
    ir, ii = inner[0], inner[1]
    copies = []
    for part in range(2):
        total = dot(pr, ii, NN) + dot(pi, ir, NN) if part else dot(pr, ir, NN) - dot(pi, ii, NN)
        back[part, :, :half] = total[:, :half].astype(BF16)
        back[part, :, half:] = (-total[:, half:]).astype(BF16)
        for place, out in enumerate((x.at[0], x.at[1], y.at[0], y.at[1])):
            columns = block(where[4 + place], width)
            copies.append(pltpu.make_async_copy(back.at[part, :, columns], out.at[part], sems.at[part, place]))
            copies[-1].start()
    for copy in copies:
        copy.wait()


def forward_kernel(where, p0, p1, p2, p3, m0, m123, kept_x, kept_y, given_x, given_y, prop, meson, ahead, total):
    width = p0.shape[-1]
    half = prop.shape[-1] // 2
    for place, p in enumerate((p0, p1, p2, p3)):
        prop[:, :, block(where[place], width)] = p[...]
    meson[:, :, block(where[4], width)] = m0[...]
    for n in range(3):
        meson[:, :, block(where[5 + n], width)] = m123[n]
    pr, pi, mr, mi = prop[0], prop[1], meson[0], meson[1]
    for part, value in ((0, dot(mr, pr, NN) - dot(mi, pi, NN)), (1, dot(mr, pi, NN) + dot(mi, pr, NN))):
        ahead[part, :half] = value[:half].astype(BF16)
        ahead[part, half:] = -value[half:].astype(BF16)
    ar, ai = ahead[0], ahead[1]
    for part, value in ((0, dot(pr, ar, TN) + dot(pi, ai, TN)), (1, dot(pr, ai, TN) - dot(pi, ar, TN))):
        total[part, :half] = value[:half]
        total[part, half:] = -value[half:]
    for n, out in enumerate((kept_x, kept_y, given_x, given_y)):
        out[...] = total[:, :, block(where[8 + n], width)]


def shards(near_prop, far_prop, meson):
    _, parts, order, width = meson.shape
    peers = lax.axis_size("tm")
    cols = lax.axis_size("col")
    steps = (peers // 8, 3 * peers // 8)
    j, q = lax.axis_index("tm"), lax.axis_index("col")
    c, k = q >> 1, q & 1

    def level(row):
        return (row >= peers // 2) * 1

    def to_rows(sign, crossed):
        pairs = []
        for row in range(peers):
            for chip in range(2):
                for core in range(2):
                    target = core ^ crossed if sign < 0 else core
                    there = (row + sign * steps[target]) % peers
                    chip_there = chip ^ level(row) ^ level(there)
                    pairs.append((row * cols + 2 * chip + core, there * cols + 2 * chip_there + (core ^ crossed)))
        return pairs

    def in_row(array, by):
        return lax.ppermute(array, "col", [(i, i ^ by) for i in range(cols)])

    def out_of_row(array, sign, crossed):
        return lax.ppermute(array, ("tm", "col"), to_rows(sign, crossed))

    ours = c ^ level(j)
    theirs = 1 - ours

    def pick(array, at):
        return lax.dynamic_index_in_dim(array, at, 0, keepdims=False)

    def prop_at(near_core, at):
        return jnp.where(k == near_core, pick(near_prop, at), pick(far_prop, at))

    m_ours, m_theirs = pick(meson, ours), pick(meson, theirs)
    p_ours, p_sib = prop_at(0, ours), prop_at(1, ours)

    p_from_sib, m_sib = in_row(jnp.stack([p_sib, m_ours]), 1)
    next_1 = out_of_row(m_ours, -1, 0)
    m_cross = in_row(m_theirs, 2)
    m_last = in_row(m_cross, 1)
    next_2 = out_of_row(jnp.stack([m_sib, m_cross, m_last]), -1, 0)
    p_cross = in_row(jnp.stack([prop_at(0, theirs), prop_at(1, theirs)]), 2)
    p_cross, next_1 = lax.optimization_barrier((p_cross, next_1))
    p_last = in_row(p_cross[1], 1)

    props = (p_ours, p_from_sib, p_cross[0], p_last)
    mesons = (m_ours, m_sib, m_cross, m_last)
    step = jnp.where(k == 0, steps[0], steps[1])
    to_chip = ours ^ level((j + step) & (peers - 1))
    x, y = 2 * (1 - to_chip), 2 * to_chip
    where_back = jnp.stack([q, q ^ 1, q ^ 2, q ^ 3, x + k, x + 1 - k, y + k, y + 1 - k]).astype(jnp.int32)
    piece = jax.ShapeDtypeStruct((2, parts, order, width), BF16)
    whole = pltpu.VMEM((parts, order, order), BF16)
    vmem, smem = pl.BlockSpec(memory_space=pltpu.VMEM), pl.BlockSpec(memory_space=pltpu.SMEM)
    product = 8 * order**3
    x_out, y_out = pl.pallas_call(
        backward_kernel,
        out_shape=[piece] * 2,
        in_specs=[smem] + [vmem] * 8,
        out_specs=[pl.BlockSpec(memory_space=pltpu.HBM)] * 2,
        scratch_shapes=[whole] * 4 + [pltpu.SemaphoreType.DMA((2, 4))],
        compiler_params=pltpu.CompilerParams(vmem_limit_bytes=24 * 2**20),
        cost_estimate=pl.CostEstimate(flops=1, bytes_accessed=1, transcendentals=0),
        name="backward",
    )(where_back, *props, *mesons)
    x_in = out_of_row(x_out, 1, 0)
    *late, x_out = lax.optimization_barrier((*props, x_out))

    u, v = 2 * to_chip, 2 * (1 - to_chip)
    z, w = 2 * (1 - c), 2 * c
    where_next = jnp.stack(
        [q, q ^ 1, q ^ 2, q ^ 3, u + k, u + 1 - k, v + k, v + 1 - k, z + k, w + k, z + 1 - k, w + 1 - k]
    ).astype(jnp.int32)
    kept_x, kept_y, given_x, given_y = pl.pallas_call(
        forward_kernel,
        out_shape=[jax.ShapeDtypeStruct((parts, order, width), F32)] * 4,
        in_specs=[smem] + [vmem] * 6,
        out_specs=[vmem] * 4,
        scratch_shapes=[whole] * 3 + [pltpu.VMEM((parts, order, order), F32)],
        compiler_params=pltpu.CompilerParams(vmem_limit_bytes=24 * 2**20),
        cost_estimate=pl.CostEstimate(flops=int(5 * product), bytes_accessed=14 * parts * order * width * 2, transcendentals=0),
        name="forward",
    )(where_next, *late, next_1, next_2)

    y_out, kept_y = lax.optimization_barrier((y_out, kept_y))
    y_in = out_of_row(y_out, 1, 0)
    from_sib = in_row((given_x + x_in[1].astype(F32)).astype(BF16), 1)
    sent = kept_x + x_in[0].astype(F32) + from_sib.astype(F32)
    sent = sent.astype(BF16)
    y_now, held = lax.optimization_barrier((y_in, sent))
    from_partner = in_row(sent, 2)
    from_sib_y = in_row((given_y + y_now[1].astype(F32)).astype(BF16), 1)
    stay = kept_y + y_in[0].astype(F32)
    stay, from_partner, from_sib_y = lax.optimization_barrier((stay, from_partner, from_sib_y))
    slot = lax.broadcasted_iota(jnp.int32, (2, parts, order, width), 0)
    return jnp.where(slot == ours, (stay + from_sib_y.astype(F32))[None], from_partner.astype(F32)[None])


def solution(mesh):
    placed = (P("tm", None, None, "col"), P("tm", None, None, "col"), P("tm", None, None, "col"))
    return jax.shard_map(
        shards, mesh=mesh, in_specs=placed, out_specs=P("tm", None, None, "col"), check_vma=False
    )
```

```python
import jax
import jax.numpy as jnp
from jax import lax
from jax.experimental import pallas as pl
from jax.experimental.pallas import tpu as pltpu
from jax.sharding import PartitionSpec as P


BF16, F32 = jnp.bfloat16, jnp.float32
NT = (((1,), (1,)), ((), ()))
NN = (((1,), (0,)), ((), ()))
TN = (((0,), (0,)), ((), ()))


def dot(a, b, dims):
    return lax.dot_general(a, b, dims, preferred_element_type=F32)


def block(at, width):
    return pl.ds(pl.multiple_of(at * width, width), width)


def backward_kernel(where, p0, p1, p2, p3, m0, m1, m2, m3, x, y, prop, meson, inner, back, sems):
    width = p0.shape[-1]
    half = prop.shape[-1] // 2
    for place, (p, m) in enumerate(((p0, m0), (p1, m1), (p2, m2), (p3, m3))):
        at = where[place]
        sign = jnp.where(at < 2, 1.0, -1.0).astype(F32)
        prop[:, :, block(at, width)] = p[...]
        meson[:, :, block(at, width)] = (m[...].astype(F32) * sign).astype(BF16)
    pr, pi, mr, mi = prop[0], prop[1], meson[0], meson[1]
    inner[0] = (dot(mr, pr, NT) + dot(mi, pi, NT)).astype(BF16)
    inner[1] = (dot(mi, pr, NT) - dot(mr, pi, NT)).astype(BF16)
    ir, ii = inner[0], inner[1]
    copies = []
    for part in range(2):
        total = dot(pr, ii, NN) + dot(pi, ir, NN) if part else dot(pr, ir, NN) - dot(pi, ii, NN)
        back[part, :, :half] = total[:, :half].astype(BF16)
        back[part, :, half:] = (-total[:, half:]).astype(BF16)
        for place, out in enumerate((x.at[0], x.at[1], y.at[0], y.at[1])):
            columns = block(where[4 + place], width)
            copies.append(pltpu.make_async_copy(back.at[part, :, columns], out.at[part], sems.at[part, place]))
            copies[-1].start()
    for copy in copies:
        copy.wait()


def forward_kernel(where, p0, p1, p2, p3, m0, m123, kept_x, kept_y, given_x, given_y, prop, meson, ahead, total):
    width = p0.shape[-1]
    half = prop.shape[-1] // 2
    for place, p in enumerate((p0, p1, p2, p3)):
        prop[:, :, block(where[place], width)] = p[...]
    meson[:, :, block(where[4], width)] = m0[...]
    for n in range(3):
        meson[:, :, block(where[5 + n], width)] = m123[n]
    pr, pi, mr, mi = prop[0], prop[1], meson[0], meson[1]
    for part, value in ((0, dot(mr, pr, NN) - dot(mi, pi, NN)), (1, dot(mr, pi, NN) + dot(mi, pr, NN))):
        ahead[part, :half] = value[:half].astype(BF16)
        ahead[part, half:] = -value[half:].astype(BF16)
    ar, ai = ahead[0], ahead[1]
    for part, value in ((0, dot(pr, ar, TN) + dot(pi, ai, TN)), (1, dot(pr, ai, TN) - dot(pi, ar, TN))):
        total[part, :half] = value[:half]
        total[part, half:] = -value[half:]
    for n, out in enumerate((kept_x, kept_y, given_x, given_y)):
        out[...] = total[:, :, block(where[8 + n], width)]


def shards(near_prop, far_prop, meson):
    _, parts, order, width = meson.shape
    peers = lax.axis_size("tm")
    cols = lax.axis_size("col")
    steps = (peers // 8, 3 * peers // 8)
    j, q = lax.axis_index("tm"), lax.axis_index("col")
    c, k = q >> 1, q & 1

    def level(row):
        return (row >= peers // 2) * 1

    def to_rows(sign, crossed):
        pairs = []
        for row in range(peers):
            for chip in range(2):
                for core in range(2):
                    target = core ^ crossed if sign < 0 else core
                    there = (row + sign * steps[target]) % peers
                    chip_there = chip ^ level(row) ^ level(there)
                    pairs.append((row * cols + 2 * chip + core, there * cols + 2 * chip_there + (core ^ crossed)))
        return pairs

    def in_row(array, by):
        return lax.ppermute(array, "col", [(i, i ^ by) for i in range(cols)])

    def out_of_row(array, sign, crossed):
        return lax.ppermute(array, ("tm", "col"), to_rows(sign, crossed))

    ours = c ^ level(j)
    theirs = 1 - ours

    def pick(array, at):
        return lax.dynamic_index_in_dim(array, at, 0, keepdims=False)

    def prop_at(near_core, at):
        return jnp.where(k == near_core, pick(near_prop, at), pick(far_prop, at))

    m_ours, m_theirs = pick(meson, ours), pick(meson, theirs)
    p_ours, p_sib = prop_at(0, ours), prop_at(1, ours)

    p_from_sib, m_sib = in_row(jnp.stack([p_sib, m_ours]), 1)
    next_1 = out_of_row(m_ours, -1, 0)
    m_cross = in_row(m_theirs, 2)
    m_last = in_row(m_cross, 1)
    next_2 = out_of_row(jnp.stack([m_sib, m_cross, m_last]), -1, 0)
    p_cross = in_row(jnp.stack([prop_at(0, theirs), prop_at(1, theirs)]), 2)
    p_cross, next_1 = lax.optimization_barrier((p_cross, next_1))
    p_last = in_row(p_cross[1], 1)

    props = (p_ours, p_from_sib, p_cross[0], p_last)
    mesons = (m_ours, m_sib, m_cross, m_last)
    step = jnp.where(k == 0, steps[0], steps[1])
    to_chip = ours ^ level((j + step) & (peers - 1))
    x, y = 2 * (1 - to_chip), 2 * to_chip
    where_back = jnp.stack([q, q ^ 1, q ^ 2, q ^ 3, x + k, x + 1 - k, y + k, y + 1 - k]).astype(jnp.int32)
    piece = jax.ShapeDtypeStruct((2, parts, order, width), BF16)
    whole = pltpu.VMEM((parts, order, order), BF16)
    vmem, smem = pl.BlockSpec(memory_space=pltpu.VMEM), pl.BlockSpec(memory_space=pltpu.SMEM)
    product = 8 * order**3
    x_out, y_out = pl.pallas_call(
        backward_kernel,
        out_shape=[piece] * 2,
        in_specs=[smem] + [vmem] * 8,
        out_specs=[pl.BlockSpec(memory_space=pltpu.HBM)] * 2,
        scratch_shapes=[whole] * 4 + [pltpu.SemaphoreType.DMA((2, 4))],
        compiler_params=pltpu.CompilerParams(vmem_limit_bytes=24 * 2**20),
        cost_estimate=pl.CostEstimate(flops=1, bytes_accessed=1, transcendentals=0),
        name="backward",
    )(where_back, *props, *mesons)
    x_in = out_of_row(x_out, 1, 0)
    y_out, next_2 = lax.optimization_barrier((y_out, next_2))
    y_in = out_of_row(y_out, 1, 0)
    *late, x_out = lax.optimization_barrier((*props, x_out))

    u, v = 2 * to_chip, 2 * (1 - to_chip)
    z, w = 2 * (1 - c), 2 * c
    where_next = jnp.stack(
        [q, q ^ 1, q ^ 2, q ^ 3, u + k, u + 1 - k, v + k, v + 1 - k, z + k, w + k, z + 1 - k, w + 1 - k]
    ).astype(jnp.int32)
    kept_x, kept_y, given_x, given_y = pl.pallas_call(
        forward_kernel,
        out_shape=[jax.ShapeDtypeStruct((parts, order, width), F32)] * 4,
        in_specs=[smem] + [vmem] * 6,
        out_specs=[vmem] * 4,
        scratch_shapes=[whole] * 3 + [pltpu.VMEM((parts, order, order), F32)],
        compiler_params=pltpu.CompilerParams(vmem_limit_bytes=24 * 2**20),
        cost_estimate=pl.CostEstimate(flops=int(5 * product), bytes_accessed=14 * parts * order * width * 2, transcendentals=0),
        name="forward",
    )(where_next, *late, next_1, next_2)

    from_sib = in_row((given_x + x_in[1].astype(F32)).astype(BF16), 1)
    sent = kept_x + x_in[0].astype(F32) + from_sib.astype(F32)
    sent = sent.astype(BF16)
    y_now, held = lax.optimization_barrier((y_in, sent))
    from_partner = in_row(sent, 2)
    from_sib_y = in_row((given_y + y_now[1].astype(F32)).astype(BF16), 1)
    stay = kept_y + y_in[0].astype(F32)
    stay, from_partner, from_sib_y = lax.optimization_barrier((stay, from_partner, from_sib_y))
    slot = lax.broadcasted_iota(jnp.int32, (2, parts, order, width), 0)
    return jnp.where(slot == ours, (stay + from_sib_y.astype(F32))[None], from_partner.astype(F32)[None])


def solution(mesh):
    placed = (P("tm", None, None, "col"), P("tm", None, None, "col"), P("tm", None, None, "col"))
    return jax.shard_map(
        shards, mesh=mesh, in_specs=placed, out_specs=P("tm", None, None, "col"), check_vma=False
    )
```

```python
import jax
import jax.numpy as jnp
from jax import lax
from jax.experimental import pallas as pl
from jax.experimental.pallas import tpu as pltpu
from jax.sharding import PartitionSpec as P


BF16, F32 = jnp.bfloat16, jnp.float32
NT = (((1,), (1,)), ((), ()))
NN = (((1,), (0,)), ((), ()))
TN = (((0,), (0,)), ((), ()))


def dot(a, b, dims):
    return lax.dot_general(a, b, dims, preferred_element_type=F32)


def block(at, width):
    return pl.ds(pl.multiple_of(at * width, width), width)


def backward_kernel(where, p0, p1, p2, p3, m0, m1, m2, m3, x, y, prop, meson, inner, back, sems):
    width = p0.shape[-1]
    half = prop.shape[-1] // 2
    for place, (p, m) in enumerate(((p0, m0), (p1, m1), (p2, m2), (p3, m3))):
        at = where[place]
        sign = jnp.where(at < 2, 1.0, -1.0).astype(F32)
        prop[:, :, block(at, width)] = p[...]
        meson[:, :, block(at, width)] = jnp.where(at < 2, m[...], -m[...])
    pr, pi, mr, mi = prop[0], prop[1], meson[0], meson[1]
    inner[0] = (dot(mr, pr, NT) + dot(mi, pi, NT)).astype(BF16)
    inner[1] = (dot(mi, pr, NT) - dot(mr, pi, NT)).astype(BF16)
    ir, ii = inner[0], inner[1]
    copies = []
    for part in range(2):
        total = dot(pr, ii, NN) + dot(pi, ir, NN) if part else dot(pr, ir, NN) - dot(pi, ii, NN)
        back[part, :, :half] = total[:, :half].astype(BF16)
        back[part, :, half:] = (-total[:, half:]).astype(BF16)
        for place, out in enumerate((x.at[0], x.at[1], y.at[0], y.at[1])):
            columns = block(where[4 + place], width)
            copies.append(pltpu.make_async_copy(back.at[part, :, columns], out.at[part], sems.at[part, place]))
            copies[-1].start()
    for copy in copies:
        copy.wait()


def forward_kernel(where, p0, p1, p2, p3, m0, m123, kept_x, kept_y, given_x, given_y, prop, meson, ahead, total):
    width = p0.shape[-1]
    half = prop.shape[-1] // 2
    for place, p in enumerate((p0, p1, p2, p3)):
        prop[:, :, block(where[place], width)] = p[...]
    meson[:, :, block(where[4], width)] = m0[...]
    for n in range(3):
        meson[:, :, block(where[5 + n], width)] = m123[n]
    pr, pi, mr, mi = prop[0], prop[1], meson[0], meson[1]
    for part, value in ((0, dot(mr, pr, NN) - dot(mi, pi, NN)), (1, dot(mr, pi, NN) + dot(mi, pr, NN))):
        ahead[part, :half] = value[:half].astype(BF16)
        ahead[part, half:] = -value[half:].astype(BF16)
    ar, ai = ahead[0], ahead[1]
    for part, value in ((0, dot(pr, ar, TN) + dot(pi, ai, TN)), (1, dot(pr, ai, TN) - dot(pi, ar, TN))):
        total[part, :half] = value[:half]
        total[part, half:] = -value[half:]
    for n, out in enumerate((kept_x, kept_y, given_x, given_y)):
        out[...] = total[:, :, block(where[8 + n], width)]


def shards(near_prop, far_prop, meson):
    _, parts, order, width = meson.shape
    peers = lax.axis_size("tm")
    cols = lax.axis_size("col")
    steps = (peers // 8, 3 * peers // 8)
    j, q = lax.axis_index("tm"), lax.axis_index("col")
    c, k = q >> 1, q & 1

    def level(row):
        return (row >= peers // 2) * 1

    def to_rows(sign, crossed):
        pairs = []
        for row in range(peers):
            for chip in range(2):
                for core in range(2):
                    target = core ^ crossed if sign < 0 else core
                    there = (row + sign * steps[target]) % peers
                    chip_there = chip ^ level(row) ^ level(there)
                    pairs.append((row * cols + 2 * chip + core, there * cols + 2 * chip_there + (core ^ crossed)))
        return pairs

    def in_row(array, by):
        return lax.ppermute(array, "col", [(i, i ^ by) for i in range(cols)])

    def out_of_row(array, sign, crossed):
        return lax.ppermute(array, ("tm", "col"), to_rows(sign, crossed))

    ours = c ^ level(j)
    theirs = 1 - ours

    def pick(array, at):
        return lax.dynamic_index_in_dim(array, at, 0, keepdims=False)

    def prop_at(near_core, at):
        return jnp.where(k == near_core, pick(near_prop, at), pick(far_prop, at))

    m_ours, m_theirs = pick(meson, ours), pick(meson, theirs)
    p_ours, p_sib = prop_at(0, ours), prop_at(1, ours)

    p_from_sib, m_sib = in_row(jnp.stack([p_sib, m_ours]), 1)
    next_1 = out_of_row(m_ours, -1, 0)
    m_cross = in_row(m_theirs, 2)
    m_last = in_row(m_cross, 1)
    next_2 = out_of_row(jnp.stack([m_sib, m_cross, m_last]), -1, 0)
    p_cross = in_row(jnp.stack([prop_at(0, theirs), prop_at(1, theirs)]), 2)
    p_cross, next_1 = lax.optimization_barrier((p_cross, next_1))
    p_last = in_row(p_cross[1], 1)

    props = (p_ours, p_from_sib, p_cross[0], p_last)
    mesons = (m_ours, m_sib, m_cross, m_last)
    step = jnp.where(k == 0, steps[0], steps[1])
    to_chip = ours ^ level((j + step) & (peers - 1))
    x, y = 2 * (1 - to_chip), 2 * to_chip
    where_back = jnp.stack([q, q ^ 1, q ^ 2, q ^ 3, x + k, x + 1 - k, y + k, y + 1 - k]).astype(jnp.int32)
    piece = jax.ShapeDtypeStruct((2, parts, order, width), BF16)
    whole = pltpu.VMEM((parts, order, order), BF16)
    vmem, smem = pl.BlockSpec(memory_space=pltpu.VMEM), pl.BlockSpec(memory_space=pltpu.SMEM)
    product = 8 * order**3
    x_out, y_out = pl.pallas_call(
        backward_kernel,
        out_shape=[piece] * 2,
        in_specs=[smem] + [vmem] * 8,
        out_specs=[pl.BlockSpec(memory_space=pltpu.HBM)] * 2,
        scratch_shapes=[whole] * 4 + [pltpu.SemaphoreType.DMA((2, 4))],
        compiler_params=pltpu.CompilerParams(vmem_limit_bytes=24 * 2**20),
        cost_estimate=pl.CostEstimate(flops=1, bytes_accessed=1, transcendentals=0),
        name="backward",
    )(where_back, *props, *mesons)
    x_in = out_of_row(x_out, 1, 0)
    y_out, next_2 = lax.optimization_barrier((y_out, next_2))
    y_in = out_of_row(y_out, 1, 0)
    *late, x_out = lax.optimization_barrier((*props, x_out))

    u, v = 2 * to_chip, 2 * (1 - to_chip)
    z, w = 2 * (1 - c), 2 * c
    where_next = jnp.stack(
        [q, q ^ 1, q ^ 2, q ^ 3, u + k, u + 1 - k, v + k, v + 1 - k, z + k, w + k, z + 1 - k, w + 1 - k]
    ).astype(jnp.int32)
    kept_x, kept_y, given_x, given_y = pl.pallas_call(
        forward_kernel,
        out_shape=[jax.ShapeDtypeStruct((parts, order, width), F32)] * 4,
        in_specs=[smem] + [vmem] * 6,
        out_specs=[vmem] * 4,
        scratch_shapes=[whole] * 3 + [pltpu.VMEM((parts, order, order), F32)],
        compiler_params=pltpu.CompilerParams(vmem_limit_bytes=24 * 2**20),
        cost_estimate=pl.CostEstimate(flops=int(5 * product), bytes_accessed=14 * parts * order * width * 2, transcendentals=0),
        name="forward",
    )(where_next, *late, next_1, next_2)

    from_sib = in_row((given_x + x_in[1].astype(F32)).astype(BF16), 1)
    sent = kept_x + x_in[0].astype(F32) + from_sib.astype(F32)
    sent = sent.astype(BF16)
    y_now, held = lax.optimization_barrier((y_in, sent))
    from_partner = in_row(sent, 2)
    from_sib_y = in_row((given_y + y_now[1].astype(F32)).astype(BF16), 1)
    stay = kept_y + y_in[0].astype(F32)
    stay, from_partner, from_sib_y = lax.optimization_barrier((stay, from_partner, from_sib_y))
    slot = lax.broadcasted_iota(jnp.int32, (2, parts, order, width), 0)
    return jnp.where(slot == ours, (stay + from_sib_y.astype(F32))[None], from_partner.astype(F32)[None])


def solution(mesh):
    placed = (P("tm", None, None, "col"), P("tm", None, None, "col"), P("tm", None, None, "col"))
    return jax.shard_map(
        shards, mesh=mesh, in_specs=placed, out_specs=P("tm", None, None, "col"), check_vma=False
    )
```

```python
import jax
import jax.numpy as jnp
from jax import lax
from jax.experimental import pallas as pl
from jax.experimental.pallas import tpu as pltpu
from jax.sharding import PartitionSpec as P


BF16, F32 = jnp.bfloat16, jnp.float32
NT = (((1,), (1,)), ((), ()))
NN = (((1,), (0,)), ((), ()))
TN = (((0,), (0,)), ((), ()))


def dot(a, b, dims):
    return lax.dot_general(a, b, dims, preferred_element_type=F32)


def block(at, width):
    return pl.ds(pl.multiple_of(at * width, width), width)


def backward_kernel(where, p0, p1, p2, p3, m0, m1, m2, m3, x, y, prop, meson, inner, back, sems):
    width = p0.shape[-1]
    half = prop.shape[-1] // 2
    for place, (p, m) in enumerate(((p0, m0), (p1, m1), (p2, m2), (p3, m3))):
        at = where[place]
        sign = jnp.where(at < 2, 1.0, -1.0).astype(F32)
        prop[:, :, block(at, width)] = p[...]
        meson[:, :, block(at, width)] = (m[...].astype(F32) * sign).astype(BF16)
    pr, pi, mr, mi = prop[0], prop[1], meson[0], meson[1]
    inner[0] = (dot(mr, pr, NT) + dot(mi, pi, NT)).astype(BF16)
    inner[1] = (dot(mi, pr, NT) - dot(mr, pi, NT)).astype(BF16)
    ir, ii = inner[0], inner[1]
    copies = []
    for part in range(2):
        total = dot(pr, ii, NN) + dot(pi, ir, NN) if part else dot(pr, ir, NN) - dot(pi, ii, NN)
        back[part, :, :half] = total[:, :half].astype(BF16)
        back[part, :, half:] = (-total[:, half:]).astype(BF16)
        for place, out in enumerate((x.at[0], x.at[1], y.at[0], y.at[1])):
            columns = block(where[4 + place], width)
            copies.append(pltpu.make_async_copy(back.at[part, :, columns], out.at[part], sems.at[part, place]))
            copies[-1].start()
    for copy in copies:
        copy.wait()


def forward_kernel(where, p0, p1, p2, p3, m0, m123, kept_x, kept_y, given_x, given_y, prop, meson, ahead, total):
    width = p0.shape[-1]
    half = prop.shape[-1] // 2
    for place, p in enumerate((p0, p1, p2, p3)):
        prop[:, :, block(where[place], width)] = p[...]
    meson[:, :, block(where[4], width)] = m0[...]
    for n in range(3):
        meson[:, :, block(where[5 + n], width)] = m123[n]
    pr, pi, mr, mi = prop[0], prop[1], meson[0], meson[1]
    for part, value in ((0, dot(mr, pr, NN) - dot(mi, pi, NN)), (1, dot(mr, pi, NN) + dot(mi, pr, NN))):
        ahead[part, :half] = value[:half].astype(BF16)
        ahead[part, half:] = -value[half:].astype(BF16)
    ar, ai = ahead[0], ahead[1]
    for part, value in ((0, dot(pr, ar, TN) + dot(pi, ai, TN)), (1, dot(pr, ai, TN) - dot(pi, ar, TN))):
        total[part, :half] = value[:half]
        total[part, half:] = -value[half:]
    for n, out in enumerate((kept_x, kept_y, given_x, given_y)):
        out[...] = total[:, :, block(where[8 + n], width)]


def shards(near_prop, far_prop, meson):
    _, parts, order, width = meson.shape
    peers = lax.axis_size("tm")
    cols = lax.axis_size("col")
    steps = (peers // 8, 3 * peers // 8)
    j, q = lax.axis_index("tm"), lax.axis_index("col")
    c, k = q >> 1, q & 1

    def level(row):
        return (row >= peers // 2) * 1

    def to_rows(sign, crossed):
        pairs = []
        for row in range(peers):
            for chip in range(2):
                for core in range(2):
                    target = core ^ crossed if sign < 0 else core
                    there = (row + sign * steps[target]) % peers
                    chip_there = chip ^ level(row) ^ level(there)
                    pairs.append((row * cols + 2 * chip + core, there * cols + 2 * chip_there + (core ^ crossed)))
        return pairs

    def in_row(array, by):
        return lax.ppermute(array, "col", [(i, i ^ by) for i in range(cols)])

    def out_of_row(array, sign, crossed):
        return lax.ppermute(array, ("tm", "col"), to_rows(sign, crossed))

    ours = c ^ level(j)
    theirs = 1 - ours

    def pick(array, at):
        return lax.dynamic_index_in_dim(array, at, 0, keepdims=False)

    def prop_at(near_core, at):
        return jnp.where(k == near_core, pick(near_prop, at), pick(far_prop, at))

    m_ours, m_theirs = jnp.where(ours == 0, meson[0], meson[1]), jnp.where(ours == 0, meson[1], meson[0])
    p_ours, p_sib = prop_at(0, ours), prop_at(1, ours)

    p_from_sib, m_sib = in_row(jnp.stack([p_sib, m_ours]), 1)
    next_1 = out_of_row(m_ours, -1, 0)
    m_cross = in_row(m_theirs, 2)
    m_last = in_row(m_cross, 1)
    next_2 = out_of_row(jnp.stack([m_sib, m_cross, m_last]), -1, 0)
    p_cross = in_row(jnp.stack([prop_at(0, theirs), prop_at(1, theirs)]), 2)
    p_cross, next_1 = lax.optimization_barrier((p_cross, next_1))
    p_last = in_row(p_cross[1], 1)

    props = (p_ours, p_from_sib, p_cross[0], p_last)
    mesons = (m_ours, m_sib, m_cross, m_last)
    step = jnp.where(k == 0, steps[0], steps[1])
    to_chip = ours ^ level((j + step) & (peers - 1))
    x, y = 2 * (1 - to_chip), 2 * to_chip
    where_back = jnp.stack([q, q ^ 1, q ^ 2, q ^ 3, x + k, x + 1 - k, y + k, y + 1 - k]).astype(jnp.int32)
    piece = jax.ShapeDtypeStruct((2, parts, order, width), BF16)
    whole = pltpu.VMEM((parts, order, order), BF16)
    vmem, smem = pl.BlockSpec(memory_space=pltpu.VMEM), pl.BlockSpec(memory_space=pltpu.SMEM)
    product = 8 * order**3
    x_out, y_out = pl.pallas_call(
        backward_kernel,
        out_shape=[piece] * 2,
        in_specs=[smem] + [vmem] * 8,
        out_specs=[pl.BlockSpec(memory_space=pltpu.HBM)] * 2,
        scratch_shapes=[whole] * 4 + [pltpu.SemaphoreType.DMA((2, 4))],
        compiler_params=pltpu.CompilerParams(vmem_limit_bytes=24 * 2**20),
        cost_estimate=pl.CostEstimate(flops=1, bytes_accessed=1, transcendentals=0),
        name="backward",
    )(where_back, *props, *mesons)
    x_in = out_of_row(x_out, 1, 0)
    y_out, next_2 = lax.optimization_barrier((y_out, next_2))
    y_in = out_of_row(y_out, 1, 0)
    *late, x_out = lax.optimization_barrier((*props, x_out))

    u, v = 2 * to_chip, 2 * (1 - to_chip)
    z, w = 2 * (1 - c), 2 * c
    where_next = jnp.stack(
        [q, q ^ 1, q ^ 2, q ^ 3, u + k, u + 1 - k, v + k, v + 1 - k, z + k, w + k, z + 1 - k, w + 1 - k]
    ).astype(jnp.int32)
    kept_x, kept_y, given_x, given_y = pl.pallas_call(
        forward_kernel,
        out_shape=[jax.ShapeDtypeStruct((parts, order, width), F32)] * 4,
        in_specs=[smem] + [vmem] * 6,
        out_specs=[vmem] * 4,
        scratch_shapes=[whole] * 3 + [pltpu.VMEM((parts, order, order), F32)],
        compiler_params=pltpu.CompilerParams(vmem_limit_bytes=24 * 2**20),
        cost_estimate=pl.CostEstimate(flops=int(5 * product), bytes_accessed=14 * parts * order * width * 2, transcendentals=0),
        name="forward",
    )(where_next, *late, next_1, next_2)

    from_sib = in_row((given_x + x_in[1].astype(F32)).astype(BF16), 1)
    sent = kept_x + x_in[0].astype(F32) + from_sib.astype(F32)
    sent = sent.astype(BF16)
    y_now, held = lax.optimization_barrier((y_in, sent))
    from_partner = in_row(sent, 2)
    from_sib_y = in_row((given_y + y_now[1].astype(F32)).astype(BF16), 1)
    stay = kept_y + y_in[0].astype(F32)
    stay, from_partner, from_sib_y = lax.optimization_barrier((stay, from_partner, from_sib_y))
    slot = lax.broadcasted_iota(jnp.int32, (2, parts, order, width), 0)
    return jnp.where(slot == ours, (stay + from_sib_y.astype(F32))[None], from_partner.astype(F32)[None])


def solution(mesh):
    placed = (P("tm", None, None, "col"), P("tm", None, None, "col"), P("tm", None, None, "col"))
    return jax.shard_map(
        shards, mesh=mesh, in_specs=placed, out_specs=P("tm", None, None, "col"), check_vma=False
    )
```
